256 devices in a mesh: freq: 64 (over z, y, core), bl: 4 (over x).
Axes of the slice: x: 4, y: 4, z: 8, core: 2. Of those that a mesh axis runs over, the one named last changes fastest.
Arguments:
- visibilities: float32 [2, 128, 2, 2048], P(None, 'freq', None, 'bl'), may hold values from -6 to 6
- coherencies: bfloat16 [2, 128, 2, 100, 2048], P(None, 'freq', None, None, 'bl'), may hold values from -0.59765625 to 0.59765625
- station_pairs: int32 [2, 2048], P(None, 'bl'), may hold values from 0 to 61, as said below
- row_flags: int32 [128, 2048], P('freq', 'bl'), may hold values 0 or 1
- gains_in: float32 [2, 128, 2, 100, 62], P(None, 'freq'), may hold values from -4 to 4
- consensus_in: float32 [2, 128, 2, 100, 62], P(None, 'freq'), may hold values from -4 to 4
- dual_in: float32 [2, 128, 2, 100, 62], P(None, 'freq'), may hold values from -2 to 2
- penalty: float32 [100], replicated, may hold values from 1 to 10
- damping: float32 [4], replicated, may hold values from 0.5 to 4
Outputs:
- gains_out: float32 [2, 128, 2, 100, 62], P(None, 'freq')
- consensus_out: float32 [2, 128, 2, 100, 62], P(None, 'freq')
- dual_out: float32 [2, 128, 2, 100, 62], P(None, 'freq')
The draws below stay inside these ranges and needn't reach their ends.
Inputs may be any that keep to these rules, and one draw needn't show every extreme that they name: `station_pairs`: each sample names two different stations.
All inputs are finite; a program needn't handle non-finite values. No bound on the sum of `row_flags` on one device may be relied on, other than what follows from the above.
Results may differ from the reference program's by a relative error of at most 0.0003.
Values sent between devices are 32-bit elements; how exact they have to be, the bound alone decides.
A program may use at most 64 MiB of HBM per device.

```python
import math
import jax
import jax.numpy as jnp
from jax import lax

STATIONS = 62
DIRS = 100
POL = 2
LM_STEPS = 4
CHANNELS = 128
ROWS = 2048


def draw_station_pairs(key, part):
    key = jax.random.fold_in(key, 11)
    first_key, second_key = jax.random.split(key)
    first = jax.random.randint(first_key, (ROWS,), 0, STATIONS)
    offset = jax.random.randint(second_key, (ROWS,), 1, STATIONS)
    second = (first + offset) % STATIONS
    first = first.at[0].set(0)
    second = second.at[0].set(STATIONS - 1)
    return jnp.stack([first, second]).astype(jnp.int32)


def set_ends(array, rng, low, high):
    extent = array.shape
    place = [jax.random.randint(jax.random.fold_in(rng, axis), (), 0, extent[axis]) for axis in range(len(extent))]
    array = array.at[tuple(place)].set(low)
    longest = extent.index(max(extent))
    place[longest] = (place[longest] + 1) % extent[longest]
    return array.at[tuple(place)].set(high)


def block_levels(key, shape, pieces, least, high):
    def one(axis_at, shards_of):
        heights = jax.random.uniform(jax.random.fold_in(jax.random.fold_in(key, 6), axis_at), (shards_of,), jnp.float32, least / len(pieces), high / len(pieces))
        return jnp.repeat(jnp.exp(heights), shape[axis_at] // shards_of).reshape((-1,) + (1,) * (len(shape) - axis_at - 1))

    factor_of = one(*pieces[0])
    for cut in pieces[1:]:
        factor_of = factor_of * one(*cut)
    return factor_of


def centred(rng, dims, deviation, limit, shards=(), held_as=jnp.bfloat16):
    level = block_levels(rng, dims, shards, -0.22, 0.18) if shards else 1.0
    result = jax.random.normal(rng, dims, jnp.float32) * deviation * level
    return jnp.minimum(jnp.maximum(result, -limit), limit).astype(held_as)


def setup_inputs(seed: int = 0) -> dict:
    seeds = jax.random.split(jax.random.key(seed), 10)
    return {
        "visibilities": centred(seeds[0], (2, CHANNELS, POL, ROWS), 1.0, 6.0, ((1, 64), (3, 4)), jnp.float32),
        "coherencies": centred(seeds[1], (2, CHANNELS, POL, DIRS, ROWS), 0.1, 0.59765625, ((1, 64), (4, 4))),
        "station_pairs": draw_station_pairs(jax.random.fold_in(seeds[9], 71), 0),
        "row_flags": set_ends((jax.random.randint(seeds[3], (CHANNELS, ROWS), 0, 8) < 7).astype(jnp.int32), jax.random.fold_in(seeds[3], 1), 0, 1),
        "gains_in": centred(seeds[4], (2, CHANNELS, POL, DIRS, STATIONS), 0.7, 4.0, ((1, 64),), jnp.float32),
        "consensus_in": centred(seeds[5], (2, CHANNELS, POL, DIRS, STATIONS), 0.7, 4.0, ((1, 64),), jnp.float32),
        "dual_in": centred(seeds[6], (2, CHANNELS, POL, DIRS, STATIONS), 0.3, 2.0, ((1, 64),), jnp.float32),
        "penalty": jnp.clip(jnp.exp(jax.random.uniform(seeds[7], (DIRS,), jnp.float32, math.log(1.0), math.log(10.0))), 1.0, 10.0),
        "damping": jnp.clip(jnp.exp(jax.random.uniform(seeds[8], (LM_STEPS,), jnp.float32, math.log(0.5), math.log(4.0))), 0.5, 4.0),
    }


HIGH = lax.Precision.HIGHEST

def bernstein(position):
    other = 1.0 - position
    return jnp.stack([other * other * other, 3.0 * position * other * other, 3.0 * position * position * other, position * position * position], axis=-1)

def gather_rows(values, one_hot):
    return jnp.einsum('...s,sr->...r', values, one_hot, precision=HIGH)

def to_stations(values, one_hot):
    return jnp.einsum('...r,sr->...s', values, one_hot, precision=HIGH)

def normal_terms(visibilities, coherencies, weight, gains, first_hot, second_hot):
    first = gather_rows(gains, first_hot)
    second = gather_rows(gains, second_hot)
    coh_re = coherencies[0].astype(jnp.float32)
    coh_im = coherencies[1].astype(jnp.float32)
    tre = coh_re * second[0] + coh_im * second[1]
    tim = coh_im * second[0] - coh_re * second[1]
    model_re = jnp.sum(first[0] * tre - first[1] * tim, axis=-2)
    model_im = jnp.sum(first[0] * tim + first[1] * tre, axis=-2)
    res_re = ((visibilities[0] - model_re) * weight)[..., None, :]
    res_im = ((visibilities[1] - model_im) * weight)[..., None, :]
    sre = coh_re * first[0] - coh_im * first[1]
    sim = coh_re * first[1] + coh_im * first[0]
    num_first = jnp.stack([res_re * tre + res_im * tim, res_im * tre - res_re * tim])
    num_second = jnp.stack([res_re * sre + res_im * sim, res_re * sim - res_im * sre])
    wide = weight[..., None, :]
    numer = to_stations(num_first, first_hot) + to_stations(num_second, second_hot)
    curv = to_stations(wide * (tre * tre + tim * tim), first_hot) + to_stations(wide * (sre * sre + sim * sim), second_hot)
    return (numer, curv)

def lm_update(gains, target, numer, curv, rate, damp):
    return gains + (numer - rate * (gains - target)) / (curv + damp + rate)

def fit_coeffs(basis_all, total):
    gram = jnp.dot(basis_all.T, basis_all, precision=HIGH)
    factor = jnp.linalg.cholesky(gram)
    flat = total.reshape(4, -1)
    forward = []
    for row in range(4):
        acc = flat[row]
        for col in range(row):
            acc = acc - factor[row, col] * forward[col]
        forward.append(acc / factor[row, row])
    backward = [None, None, None, None]
    for row in range(3, -1, -1):
        acc = forward[row]
        for col in range(row + 1, 4):
            acc = acc - factor[col, row] * backward[col]
        backward[row] = acc / factor[row, row]
    return jnp.stack(backward).reshape(total.shape)

def reference(visibilities, coherencies, station_pairs, row_flags, gains_in, consensus_in, dual_in, penalty, damping):
    station_ids = lax.broadcasted_iota(jnp.int32, (STATIONS, ROWS), 0)
    first_hot = (station_ids == station_pairs[0][None, :]).astype(jnp.float32)
    second_hot = (station_ids == station_pairs[1][None, :]).astype(jnp.float32)
    target = consensus_in - dual_in
    rate = penalty[:, None]

    def per_channel(items):
        vis_c, coh_c, flag_c, gains, target_c = items
        weight = flag_c.astype(jnp.float32)
        for step in range(LM_STEPS):
            numer, curv = normal_terms(vis_c, coh_c, weight, gains, first_hot, second_hot)
            gains = lm_update(gains, target_c, numer, curv, rate, damping[step])
        return gains
    solved = lax.map(per_channel, (jnp.moveaxis(visibilities, 1, 0), jnp.moveaxis(coherencies, 1, 0), row_flags, jnp.moveaxis(gains_in, 1, 0), jnp.moveaxis(target, 1, 0)))
    gains_out = jnp.moveaxis(solved, 0, 1)
    position = (lax.iota(jnp.int32, CHANNELS).astype(jnp.float32) + 0.5) / CHANNELS
    basis = bernstein(position)
    partial_value = jnp.einsum('fm,cfpks->mcpks', basis, gains_out + dual_in, precision=HIGH)
    coeffs = fit_coeffs(basis, partial_value)
    consensus_out = jnp.einsum('fm,mcpks->cfpks', basis, coeffs, precision=HIGH)
    dual_out = dual_in + gains_out - consensus_out
    return (gains_out, consensus_out, dual_out)
```

```python
import functools

import jax
import jax.numpy as jnp
import numpy as np
from jax import lax
from jax.experimental import pallas as pl
from jax.experimental.pallas import tpu as pltpu
from jax.sharding import PartitionSpec as P

MESH = pl.DeviceIdType.MESH
OFFSETS = (0, 1, 3, 2)
HALF = 64
WIDE = 256


def bernstein(position):
    other = 1.0 - position
    return np.stack(
        [
            other * other * other,
            3.0 * position * other * other,
            3.0 * position * position * other,
            position * position * position,
        ],
        axis=-1,
    )


def kernel(
    freqs,
    vis,
    coh,
    pairs,
    flags,
    gains_in,
    cons_in,
    dual_in,
    penalty,
    damping,
    gains_out,
    cons_out,
    dual_out,
    send_coh,
    coh_all,
    send_aux,
    aux_all,
    hot,
    hot_t,
    picked,
    terms,
    sums,
    gains,
    target,
    dual,
    rate,
    table,
    pad,
    gains_all,
    fwd_src,
    fwd_all,
    part_src,
    part_in,
    back_src,
    cons_mine,
    cons_other,
    packed,
    coh_send,
    coh_recv,
    aux_send,
    aux_recv,
    gain_send,
    gain_recv,
    misc,
):
    dirs, stations = gains_in.shape[-2:]
    rows = coh.shape[-1]
    ktiles = gains.shape[0] // 8
    owners, per_owner = fwd_src.shape[:2]
    me = lax.axis_index("freq")
    lane = lax.axis_index("bl")
    group = len(OFFSETS)

    def place(problem):
        return lax.rem(problem, 2), problem // 2

    barrier = pltpu.get_barrier_semaphore()

    def greet(step, carry):
        other = lax.rem(me + step, freqs)
        pl.semaphore_signal(barrier, inc=1, device_id={"freq": other}, device_id_type=MESH)
        return carry

    for off in OFFSETS[1:]:
        other = lax.rem(lane + off, group)
        pl.semaphore_signal(barrier, inc=1, device_id={"bl": other}, device_id_type=MESH)
    lax.fori_loop(1, freqs, greet, 0)

    def fill(off, coh_to, aux_to):
        chan, pol = place(lax.rem(lane + off, group))
        weight = flags[pl.ds(chan, 1), :].astype(jnp.float32)
        for part in range(2):
            base = part * ktiles * 8
            coh_to[base : base + dirs, :] = coh[part, chan, pol].astype(jnp.float32) * weight
            if ktiles * 8 > dirs:
                coh_to[base + dirs : base + ktiles * 8, :] = jnp.zeros((ktiles * 8 - dirs, rows), jnp.float32)
            aux_to[part : part + 1, :] = vis[part, chan, pl.ds(pol, 1), :] * weight
            aux_to[2 + part : 3 + part, :] = pairs[part : part + 1, :].astype(jnp.float32)
        aux_to[4:8, :] = jnp.zeros((4, rows), jnp.float32)

    def coh_copy(slot, off):
        return pltpu.make_async_remote_copy(
            src_ref=send_coh.at[slot - 1],
            dst_ref=coh_all.at[slot],
            send_sem=coh_send.at[slot],
            recv_sem=coh_recv.at[slot],
            device_id={"bl": lax.rem(lane + off, group)},
            device_id_type=MESH,
        )

    def aux_copy(slot, off):
        return pltpu.make_async_remote_copy(
            src_ref=send_aux.at[slot - 1],
            dst_ref=aux_all.at[slot],
            send_sem=aux_send.at[slot],
            recv_sem=aux_recv.at[slot],
            device_id={"bl": lax.rem(lane + off, group)},
            device_id_type=MESH,
        )

    for slot in range(1, group):
        fill(OFFSETS[slot], send_coh.at[slot - 1], send_aux.at[slot - 1])
    pl.semaphore_wait(barrier, freqs - 1 + group - 1)
    for slot in range(1, group):
        aux_copy(slot, OFFSETS[slot]).start()
    for slot in range(1, group):
        coh_copy(slot, OFFSETS[slot]).start()
    fill(0, coh_all.at[0], aux_all.at[0])

    lanes = lax.broadcasted_iota(jnp.int32, (8 * ktiles, 2 * HALF), 1)
    low = lanes < HALF
    chan, pol = place(lane)
    pad[...] = jnp.zeros_like(pad)

    def pack(ref):
        pad[0:dirs, 0:stations] = ref[0, chan, pol]
        real = pad[...]
        pad[0:dirs, 0:stations] = ref[1, chan, pol]
        return real + pltpu.roll(pad[...], HALF, 1)

    start = pack(gains_in)
    mine = pack(dual_in)
    gains[...] = start
    dual[...] = mine
    target[...] = pack(cons_in) - mine
    pad[0:1, 0:dirs] = penalty[...]
    lane_row = lax.broadcasted_iota(jnp.int32, (1, 2 * HALF), 1)
    spread = jnp.broadcast_to(jnp.where(lane_row < dirs, pad[0:1, :], 0.0), (2 * HALF, 2 * HALF))
    rate[...] = spread.T[0 : 8 * ktiles, :]

    def hots(slot):
        ids = lax.broadcasted_iota(jnp.int32, (2 * HALF, rows), 0)
        ids = jnp.where(ids >= HALF, ids - HALF, ids).astype(jnp.float32)
        for part in range(2):
            ones = jnp.where(ids == aux_all[slot, 2 + part : 3 + part, :], 1.0, 0.0)
            hot[slot, :, part * rows : (part + 1) * rows] = ones.astype(jnp.bfloat16)
            hot_t[slot, part * rows : (part + 1) * rows, :] = ones.T.astype(jnp.bfloat16)

    def spread_table():
        value = gains[...]
        high = value.astype(jnp.bfloat16).astype(jnp.float32)
        rest = value - high
        real = jnp.where(low, high, pltpu.roll(rest, HALF, 1))
        imag = jnp.where(low, pltpu.roll(high, HALF, 1), rest)
        for k in range(ktiles):
            both = jnp.concatenate([real[8 * k : 8 * k + 8], imag[8 * k : 8 * k + 8]], axis=0)
            table[16 * k : 16 * k + 16, :] = both.astype(jnp.bfloat16)

    def accumulate(slot):
        picked[...] = jnp.dot(table[...], hot[slot], preferred_element_type=jnp.float32)
        for at in range(0, rows, WIDE):
            first = slice(at, at + WIDE)
            second = slice(rows + at, rows + at + WIDE)

            def load(k):
                cre = coh_all[slot, 8 * k : 8 * k + 8, first]
                cim = coh_all[slot, 8 * (ktiles + k) : 8 * (ktiles + k) + 8, first]
                pre = picked[16 * k : 16 * k + 8, first]
                pim = picked[16 * k + 8 : 16 * k + 16, first]
                qre = picked[16 * k : 16 * k + 8, second]
                qim = picked[16 * k + 8 : 16 * k + 16, second]
                return cre, cim, pre, pim, qre, qim

            mre = jnp.zeros((8, WIDE), jnp.float32)
            mim = jnp.zeros((8, WIDE), jnp.float32)
            for k in range(ktiles):
                cre, cim, pre, pim, qre, qim = load(k)
                tre = cre * qre + cim * qim
                tim = cim * qre - cre * qim
                mre = mre + (pre * tre - pim * tim)
                mim = mim + (pre * tim + pim * tre)
            rre = aux_all[slot, 0:1, first] - jnp.sum(mre, axis=0, keepdims=True)
            rim = aux_all[slot, 1:2, first] - jnp.sum(mim, axis=0, keepdims=True)
            rre = jnp.broadcast_to(rre, (8, WIDE))
            rim = jnp.broadcast_to(rim, (8, WIDE))
            held = [None, None]
            for k in range(ktiles):
                cre, cim, pre, pim, qre, qim = load(k)
                are = rre * cre + rim * cim
                aim = rim * cre - rre * cim
                square = cre * cre + cim * cim
                sides = (
                    (first, are * qre - aim * qim, are * qim + aim * qre, square * (qre * qre + qim * qim)),
                    (second, are * pre + aim * pim, are * pim - aim * pre, square * (pre * pre + pim * pim)),
                )
                for side, (cols, real, imag, curv) in enumerate(sides):
                    both = jnp.concatenate([real, imag], axis=0)
                    high = both.astype(jnp.bfloat16)
                    terms[32 * k : 32 * k + 16, cols] = high
                    terms[32 * k + 16 : 32 * k + 32, cols] = (both - high.astype(jnp.float32)).astype(jnp.bfloat16)
                    base = 32 * ktiles + 8 * (k - k % 2)
                    if k % 2:
                        both = jnp.concatenate([held[side], curv], axis=0)
                        terms[base : base + 16, cols] = both.astype(jnp.bfloat16)
                    elif k == ktiles - 1:
                        both = jnp.concatenate([curv, jnp.zeros_like(curv)], axis=0)
                        terms[base : base + 16, cols] = both.astype(jnp.bfloat16)
                    held[side] = curv
        sums[...] += jnp.dot(terms[...], hot_t[slot], preferred_element_type=jnp.float32)

    def update(damp):
        half = lax.broadcasted_iota(jnp.int32, (8, 2 * HALF), 1) < HALF
        for k in range(ktiles):
            at = slice(8 * k, 8 * k + 8)
            real = sums[32 * k : 32 * k + 8, :] + sums[32 * k + 16 : 32 * k + 24, :]
            imag = sums[32 * k + 8 : 32 * k + 16, :] + sums[32 * k + 24 : 32 * k + 32, :]
            numer = jnp.where(half, real, imag)
            curv = sums[32 * ktiles + 8 * k : 32 * ktiles + 8 * k + 8, :]
            value = gains[at, :]
            pull = rate[at, :]
            gains[at, :] = value + (numer - pull * (value - target[at, :])) / (curv + damp + pull)

    def one_step(step, carry):
        spread_table()
        sums[...] = jnp.zeros_like(sums)

        def one_slot(slot, inner):
            @pl.when(step == 0)
            def _():
                @pl.when(slot > 0)
                def _():
                    aux_copy(slot, 0).wait_recv()
                hots(slot)

                @pl.when(slot > 0)
                def _():
                    coh_copy(slot, 0).wait_recv()

            accumulate(slot)
            return inner

        lax.fori_loop(0, group, one_slot, 0)
        update(damping[step])
        return carry

    lax.fori_loop(0, damping.shape[0], one_step, 0)

    blend = gains[...] + dual[...]
    for owner in range(owners):
        count = min(per_owner, dirs - owner * per_owner)
        fwd_src[owner, 0:count, :] = blend[owner * per_owner : owner * per_owner + count, :]
        if count < per_owner:
            fwd_src[owner, count:per_owner, :] = jnp.zeros((per_owner - count, 2 * HALF), jnp.float32)

    def fwd_copy(other):
        return pltpu.make_async_remote_copy(
            src_ref=fwd_src.at[other],
            dst_ref=fwd_all.at[me],
            send_sem=misc.at[0],
            recv_sem=misc.at[1],
            device_id={"freq": other},
            device_id_type=MESH,
        )

    def send_fwd(step, carry):
        other = lax.rem(me + step, freqs)

        @pl.when(other < owners)
        def _():
            fwd_copy(other).start()

        return carry

    lax.fori_loop(1, freqs, send_fwd, 0)

    def gain_copy(slot, off):
        return pltpu.make_async_remote_copy(
            src_ref=gains,
            dst_ref=gains_all.at[slot],
            send_sem=gain_send.at[slot],
            recv_sem=gain_recv.at[slot],
            device_id={"bl": lax.rem(lane + off, group)},
            device_id_type=MESH,
        )

    for slot in range(1, group):
        gain_copy(slot, OFFSETS[slot]).start()
    gains_all[0] = gains[...]

    def wait_bytes(ref, count, sem):
        view = ref.at[0:count]
        pltpu.make_async_copy(view, view, sem).wait()

    total = 2 * freqs
    basis = bernstein((np.arange(total) + 0.5) / total)
    factor = np.linalg.cholesky(basis.T @ basis)
    is_owner = me < owners

    def part_copy():
        return pltpu.make_async_remote_copy(
            src_ref=part_src,
            dst_ref=part_in,
            send_sem=misc.at[2],
            recv_sem=misc.at[3],
            device_id={"bl": lane + 1 - 2 * lax.rem(lane, 2)},
            device_id_type=MESH,
        )

    def back_copy(other):
        return pltpu.make_async_remote_copy(
            src_ref=back_src.at[other],
            dst_ref=cons_mine.at[me],
            send_sem=misc.at[4],
            recv_sem=misc.at[5],
            device_id={"freq": other},
            device_id_type=MESH,
        )

    @pl.when(is_owner)
    def _():
        fwd_all[me] = fwd_src[me]
        wait_bytes(fwd_all, freqs - 1, misc.at[1])
        for odd in range(2):

            @pl.when(chan == odd)
            def _():
                acc = [None] * 4
                for f in range(freqs):
                    value = fwd_all[f]
                    for m in range(4):
                        term = value * float(basis[2 * f + odd, m])
                        acc[m] = term if acc[m] is None else acc[m] + term
                for m in range(4):
                    part_src[m] = acc[m]

        part_copy().start()
        part_copy().wait_recv()
        whole = [part_src[m] + part_in[m] for m in range(4)]
        forward = []
        for row in range(4):
            acc = whole[row]
            for col in range(row):
                acc = acc - float(factor[row, col]) * forward[col]
            forward.append(acc * float(1.0 / factor[row, row]))
        coeffs = [None] * 4
        for row in range(3, -1, -1):
            acc = forward[row]
            for col in range(row + 1, 4):
                acc = acc - float(factor[col, row]) * coeffs[col]
            coeffs[row] = acc * float(1.0 / factor[row, row])
        for f in range(freqs):
            for odd in range(2):
                value = coeffs[0] * float(basis[2 * f + odd, 0])
                for m in range(1, 4):
                    value = value + coeffs[m] * float(basis[2 * f + odd, m])
                back_src[f, odd] = value

        def send_back(step, carry):
            back_copy(lax.rem(me + step, freqs)).start()
            return carry

        lax.fori_loop(1, freqs, send_back, 0)
        cons_mine[me] = back_src[me]
        wait_bytes(cons_mine, owners - 1, misc.at[5])

    @pl.when(jnp.logical_not(is_owner))
    def _():
        wait_bytes(cons_mine, owners, misc.at[5])

    swap = pltpu.make_async_remote_copy(
        src_ref=cons_mine,
        dst_ref=cons_other,
        send_sem=misc.at[6],
        recv_sem=misc.at[7],
        device_id={"bl": group - 1 - lane},
        device_id_type=MESH,
    )
    swap.start()

    for slot in range(1, group):
        gain_copy(slot, OFFSETS[slot]).wait_recv()

    def unpack(held, index):
        for odd in range(2):
            for owner in range(owners):
                count = min(per_owner, dirs - owner * per_owner)
                at = slice(owner * per_owner, owner * per_owner + count)
                packed[index, odd, at, :] = held[owner, odd, 0:count, :]

    def emit(slot, index):
        problem = lax.rem(lane + group - OFFSETS[slot], group)
        chan_of, pol_of = place(problem)
        solved = gains_all[slot]
        fitted = packed[index, chan_of]
        for part in range(2):
            if part:
                solved = pltpu.roll(solved, HALF, 1)
                fitted = pltpu.roll(fitted, HALF, 1)
            g = solved[0:dirs, 0:stations]
            c = fitted[0:dirs, 0:stations]
            gains_out[part, chan_of, pol_of] = g
            cons_out[part, chan_of, pol_of] = c
            dual_out[part, chan_of, pol_of] = dual_in[part, chan_of, pol_of] + g - c

    unpack(cons_mine, 0)
    emit(0, 0)
    swap.wait_recv()
    unpack(cons_other, 1)
    for slot in range(1, group):
        problem = lax.rem(lane + group - OFFSETS[slot], group)
        emit(slot, jnp.where(problem // 2 == pol, 0, 1))

    for slot in range(1, group):
        coh_copy(slot, OFFSETS[slot]).wait_send()
        aux_copy(slot, OFFSETS[slot]).wait_send()
        gain_copy(slot, OFFSETS[slot]).wait_send()
    swap.wait_send()

    @pl.when(is_owner)
    def _():
        wait_bytes(fwd_src, owners - 1, misc.at[0])
        part_copy().wait_send()
        wait_bytes(back_src, freqs - 1, misc.at[4])

    @pl.when(jnp.logical_not(is_owner))
    def _():
        wait_bytes(fwd_src, owners, misc.at[0])


def solution(mesh):
    freqs = mesh.shape["freq"]

    def step(vis, coh, pairs, flags, gains_in, cons_in, dual_in, penalty, damping):
        dirs = gains_in.shape[-2]
        rows = coh.shape[-1]
        ktiles = -(-dirs // 8)
        krows = 8 * ktiles
        term_rows = 32 * ktiles + 16 * (-(-ktiles // 2))
        group = len(OFFSETS)
        per_owner = -(-dirs // freqs)
        owners = -(-dirs // per_owner)
        lanes = 2 * HALF
        f32, b16 = jnp.float32, jnp.bfloat16
        whole = pl.BlockSpec(memory_space=pltpu.VMEM)
        scratch = [
            pltpu.VMEM((group - 1, 2 * krows, rows), f32),
            pltpu.VMEM((group, 2 * krows, rows), f32),
            pltpu.VMEM((group - 1, 8, rows), f32),
            pltpu.VMEM((group, 8, rows), f32),
            pltpu.VMEM((group, lanes, 2 * rows), b16),
            pltpu.VMEM((group, 2 * rows, lanes), b16),
            pltpu.VMEM((2 * krows, 2 * rows), f32),
            pltpu.VMEM((term_rows, 2 * rows), b16),
            pltpu.VMEM((term_rows, lanes), f32),
            pltpu.VMEM((krows, lanes), f32),
            pltpu.VMEM((krows, lanes), f32),
            pltpu.VMEM((krows, lanes), f32),
            pltpu.VMEM((krows, lanes), f32),
            pltpu.VMEM((2 * krows, lanes), b16),
            pltpu.VMEM((krows, lanes), f32),
            pltpu.VMEM((group, krows, lanes), f32),
            pltpu.VMEM((owners, per_owner, lanes), f32),
            pltpu.VMEM((freqs, per_owner, lanes), f32),
            pltpu.VMEM((4, per_owner, lanes), f32),
            pltpu.VMEM((4, per_owner, lanes), f32),
            pltpu.VMEM((freqs, 2, per_owner, lanes), f32),
            pltpu.VMEM((owners, 2, per_owner, lanes), f32),
            pltpu.VMEM((owners, 2, per_owner, lanes), f32),
            pltpu.VMEM((2, 2, krows, lanes), f32),
        ] + [pltpu.SemaphoreType.DMA((n,)) for n in (group, group, group, group, group, group, 8)]
        out = jax.ShapeDtypeStruct(gains_in.shape, f32)
        return pl.pallas_call(
            functools.partial(kernel, freqs),
            out_shape=(out, out, out),
            in_specs=[whole] * 8 + [pl.BlockSpec(memory_space=pltpu.SMEM)],
            out_specs=(whole, whole, whole),
            scratch_shapes=scratch,
            compiler_params=pltpu.CompilerParams(
                collective_id=0, has_side_effects=True, vmem_limit_bytes=40 * 1024 * 1024
            ),
        )(vis, coh, pairs, flags, gains_in, cons_in, dual_in, penalty.reshape(1, dirs), damping)

    spread = P(None, "freq", None, None, None)
    return jax.shard_map(
        step,
        mesh=mesh,
        in_specs=(
            P(None, "freq", None, "bl"),
            P(None, "freq", None, None, "bl"),
            P(None, "bl"),
            P("freq", "bl"),
            spread,
            spread,
            spread,
            P(),
            P(),
        ),
        out_specs=(spread, spread, spread),
        check_vma=False,
    )
```

```python
import functools

import jax
import jax.numpy as jnp
import numpy as np
from jax import lax
from jax.experimental import pallas as pl
from jax.experimental.pallas import tpu as pltpu
from jax.sharding import PartitionSpec as P

MESH = pl.DeviceIdType.MESH
OFFSETS = (0, 1, 3, 2)
HALF = 64
WIDE = 256


def bernstein(position):
    other = 1.0 - position
    return np.stack(
        [
            other * other * other,
            3.0 * position * other * other,
            3.0 * position * position * other,
            position * position * position,
        ],
        axis=-1,
    )


def kernel(
    freqs,
    vis,
    coh,
    pairs,
    flags,
    gains_in,
    cons_in,
    dual_in,
    penalty,
    damping,
    gains_out,
    cons_out,
    dual_out,
    send_coh,
    coh_all,
    send_aux,
    aux_all,
    hot,
    hot_t,
    picked,
    terms,
    sums,
    gains,
    target,
    dual,
    rate,
    table,
    pad,
    gains_all,
    fwd_src,
    fwd_all,
    part_src,
    part_in,
    back_src,
    cons_all,
    coh_send,
    coh_recv,
    aux_send,
    aux_recv,
    gain_send,
    gain_recv,
    back_recv,
    misc,
):
    stations, dirs = gains_in.shape[2], gains_in.shape[4]
    rows = coh.shape[-1]
    ktiles = gains.shape[0] // 8
    per_owner = HALF // freqs
    plane = min(8, freqs)
    planes = freqs // plane
    even = dirs // 8 * 8
    rest = dirs - even
    me = lax.axis_index("freq")
    lane = lax.axis_index("bl")
    group = len(OFFSETS)

    def place(problem):
        return lax.rem(problem, 2), problem // 2

    barrier = pltpu.get_barrier_semaphore()

    def greet(step, carry):
        other = lax.rem(me + step, freqs)
        pl.semaphore_signal(barrier, inc=1, device_id={"freq": other}, device_id_type=MESH)
        return carry

    for off in OFFSETS[1:]:
        other = lax.rem(lane + off, group)
        pl.semaphore_signal(barrier, inc=1, device_id={"bl": other}, device_id_type=MESH)
    lax.fori_loop(1, freqs, greet, 0)

    def fill(off, coh_to, aux_to):
        chan, pol = place(lax.rem(lane + off, group))
        weight = flags[pl.ds(chan, 1), :].astype(jnp.float32)
        for part in range(2):
            value = coh[part, chan, pol].astype(jnp.float32) * weight
            coh_to[part * even : (part + 1) * even, :] = value[0:even]
            coh_to[2 * even + part * rest : 2 * even + (part + 1) * rest, :] = value[even:dirs]
            aux_to[part : part + 1, :] = vis[part, chan, pl.ds(pol, 1), :] * weight
            aux_to[2 + part : 3 + part, :] = pairs[part : part + 1, :].astype(jnp.float32)

    def coh_copy(slot, off):
        return pltpu.make_async_remote_copy(
            src_ref=send_coh.at[slot - 1],
            dst_ref=coh_all.at[slot],
            send_sem=coh_send.at[slot],
            recv_sem=coh_recv.at[slot],
            device_id={"bl": lax.rem(lane + off, group)},
            device_id_type=MESH,
        )

    def aux_copy(slot, off):
        return pltpu.make_async_remote_copy(
            src_ref=send_aux.at[slot - 1],
            dst_ref=aux_all.at[slot],
            send_sem=aux_send.at[slot],
            recv_sem=aux_recv.at[slot],
            device_id={"bl": lax.rem(lane + off, group)},
            device_id_type=MESH,
        )

    for slot in range(1, group):
        fill(OFFSETS[slot], send_coh.at[slot - 1], send_aux.at[slot - 1])
    pl.semaphore_wait(barrier, freqs - 1 + group - 1)
    for slot in range(1, group):
        aux_copy(slot, OFFSETS[slot]).start()
    for slot in range(1, group):
        coh_copy(slot, OFFSETS[slot]).start()
    fill(0, coh_all.at[0], aux_all.at[0])

    lanes = lax.broadcasted_iota(jnp.int32, (8 * ktiles, 2 * HALF), 1)
    low = lanes < HALF
    chan, pol = place(lane)

    def pack(ref, to):
        to[...] = jnp.zeros_like(to)
        for part in range(2):
            for n in range(stations):
                to[part * HALF + n : part * HALF + n + 1, 0:dirs] = ref[part, chan, n, pl.ds(pol, 1), :]

    pack(gains_in, pad)
    gains[...] = pad[...].T[0 : 8 * ktiles, :]
    pack(dual_in, dual)
    pack(cons_in, pad)
    target[...] = (pad[...] - dual[...]).T[0 : 8 * ktiles, :]
    pad[...] = jnp.zeros_like(pad)
    pad[0:1, 0:dirs] = penalty[...]
    rate[...] = jnp.broadcast_to(pad[0:1, :], (2 * HALF, 2 * HALF)).T[0 : 8 * ktiles, :]

    def hots(slot):
        ids = lax.broadcasted_iota(jnp.int32, (2 * HALF, rows), 0)
        ids = jnp.where(ids >= HALF, ids - HALF, ids).astype(jnp.float32)
        for part in range(2):
            ones = jnp.where(ids == aux_all[slot, 2 + part : 3 + part, :], 1.0, 0.0)
            hot[slot, :, part * rows : (part + 1) * rows] = ones.astype(jnp.bfloat16)
            hot_t[slot, part * rows : (part + 1) * rows, :] = ones.T.astype(jnp.bfloat16)

    def spread_table():
        value = gains[...]
        high = value.astype(jnp.bfloat16).astype(jnp.float32)
        rest = value - high
        real = jnp.where(low, high, pltpu.roll(rest, HALF, 1))
        imag = jnp.where(low, pltpu.roll(high, HALF, 1), rest)
        for k in range(ktiles):
            both = jnp.concatenate([real[8 * k : 8 * k + 8], imag[8 * k : 8 * k + 8]], axis=0)
            table[16 * k : 16 * k + 16, :] = both.astype(jnp.bfloat16)

    def gather(slot):
        picked[slot] = jnp.dot(table[...], hot[slot], preferred_element_type=jnp.float32)

    def vector(slot):
        for at in range(0, rows, WIDE):
            first = slice(at, at + WIDE)
            second = slice(rows + at, rows + at + WIDE)

            def load(k):
                if 8 * k < even:
                    cre = coh_all[slot, 8 * k : 8 * k + 8, first]
                    cim = coh_all[slot, even + 8 * k : even + 8 * k + 8, first]
                else:
                    cre = coh_all[slot, 2 * even : 2 * even + 8, first]
                    cim = pltpu.roll(cre, rest, 0)
                pre = picked[slot, 16 * k : 16 * k + 8, first]
                pim = picked[slot, 16 * k + 8 : 16 * k + 16, first]
                qre = picked[slot, 16 * k : 16 * k + 8, second]
                qim = picked[slot, 16 * k + 8 : 16 * k + 16, second]
                return cre, cim, pre, pim, qre, qim

            mre = jnp.zeros((8, WIDE), jnp.float32)
            mim = jnp.zeros((8, WIDE), jnp.float32)
            for k in range(ktiles):
                cre, cim, pre, pim, qre, qim = load(k)
                tre = cre * qre + cim * qim
                tim = cim * qre - cre * qim
                mre = mre + (pre * tre - pim * tim)
                mim = mim + (pre * tim + pim * tre)
            rre = aux_all[slot, 0:1, first] - jnp.sum(mre, axis=0, keepdims=True)
            rim = aux_all[slot, 1:2, first] - jnp.sum(mim, axis=0, keepdims=True)
            rre = jnp.broadcast_to(rre, (8, WIDE))
            rim = jnp.broadcast_to(rim, (8, WIDE))
            held = [None, None]
            for k in range(ktiles):
                cre, cim, pre, pim, qre, qim = load(k)
                are = rre * cre + rim * cim
                aim = rim * cre - rre * cim
                square = cre * cre + cim * cim
                sides = (
                    (first, are * qre - aim * qim, are * qim + aim * qre, square * (qre * qre + qim * qim)),
                    (second, are * pre + aim * pim, are * pim - aim * pre, square * (pre * pre + pim * pim)),
                )
                for side, (cols, real, imag, curv) in enumerate(sides):
                    both = jnp.concatenate([real, imag], axis=0)
                    high = both.astype(jnp.bfloat16)
                    terms[slot, 32 * k : 32 * k + 16, cols] = high
                    terms[slot, 32 * k + 16 : 32 * k + 32, cols] = (both - high.astype(jnp.float32)).astype(jnp.bfloat16)
                    base = 32 * ktiles + 8 * (k - k % 2)
                    if k % 2:
                        both = jnp.concatenate([held[side], curv], axis=0)
                        terms[slot, base : base + 16, cols] = both.astype(jnp.bfloat16)
                    elif k == ktiles - 1:
                        both = jnp.concatenate([curv, jnp.zeros_like(curv)], axis=0)
                        terms[slot, base : base + 16, cols] = both.astype(jnp.bfloat16)
                    held[side] = curv

    def scatter(slot):
        sums[...] += jnp.dot(terms[slot], hot_t[slot], preferred_element_type=jnp.float32)

    def update(damp):
        half = lax.broadcasted_iota(jnp.int32, (8, 2 * HALF), 1) < HALF
        for k in range(ktiles):
            at = slice(8 * k, 8 * k + 8)
            real = sums[32 * k : 32 * k + 8, :] + sums[32 * k + 16 : 32 * k + 24, :]
            imag = sums[32 * k + 8 : 32 * k + 16, :] + sums[32 * k + 24 : 32 * k + 32, :]
            numer = jnp.where(half, real, imag)
            curv = sums[32 * ktiles + 8 * k : 32 * ktiles + 8 * k + 8, :]
            value = gains[at, :]
            pull = rate[at, :]
            gains[at, :] = value + (numer - pull * (value - target[at, :])) / (curv + damp + pull)

    def one_step(step, carry):
        spread_table()
        sums[...] = jnp.zeros_like(sums)
        for slot in range(group):
            gather(slot)
        for slot in range(group):
            vector(slot)
            scatter(slot)
        update(damping[step])
        return carry

    spread_table()
    sums[...] = jnp.zeros_like(sums)
    for slot in range(group):
        if slot:
            aux_copy(slot, 0).wait_recv()
        hots(slot)
        gather(slot)
        if slot:
            coh_copy(slot, 0).wait_recv()
        vector(slot)
        scatter(slot)
    update(damping[0])
    lax.fori_loop(1, damping.shape[0], one_step, 0)

    pad[0 : 8 * ktiles, :] = gains[...]
    pad[8 * ktiles : 2 * HALF, :] = jnp.zeros((2 * HALF - 8 * ktiles, 2 * HALF), jnp.float32)
    solved = pad[...].T
    gains_all[lane] = solved
    blend = solved + dual[...]
    for owner in range(freqs):
        for part in range(2):
            base = part * HALF + owner * per_owner
            fwd_src[owner, part * per_owner : (part + 1) * per_owner, :] = blend[base : base + per_owner, :]

    def far_first(send):
        here = me // plane
        order = sorted(range(planes), key=lambda d: -min(d, planes - d))
        for ahead in order:
            base = lax.rem(here + ahead, planes) * plane

            def one(step, carry):
                send(base + lax.rem(me + step, plane))
                return carry

            lax.fori_loop(0 if ahead else 1, plane, one, 0)

    def fwd_copy(other):
        return pltpu.make_async_remote_copy(
            src_ref=fwd_src.at[other],
            dst_ref=fwd_all.at[me],
            send_sem=misc.at[0],
            recv_sem=misc.at[1],
            device_id={"freq": other},
            device_id_type=MESH,
        )

    far_first(lambda other: fwd_copy(other).start())

    def gain_copy(slot, off):
        return pltpu.make_async_remote_copy(
            src_ref=gains_all.at[lane],
            dst_ref=gains_all.at[lane],
            send_sem=gain_send.at[slot],
            recv_sem=gain_recv.at[slot],
            device_id={"bl": lax.rem(lane + off, group)},
            device_id_type=MESH,
        )

    for slot in range(1, group):
        gain_copy(slot, OFFSETS[slot]).start()

    def wait_bytes(ref, count, sem):
        view = ref.at[0:count]
        pltpu.make_async_copy(view, view, sem).wait()

    total = 2 * freqs
    basis = bernstein((np.arange(total) + 0.5) / total)
    factor = np.linalg.cholesky(basis.T @ basis)

    def part_copy():
        return pltpu.make_async_remote_copy(
            src_ref=part_src,
            dst_ref=part_in,
            send_sem=misc.at[2],
            recv_sem=misc.at[3],
            device_id={"bl": lane + 1 - 2 * lax.rem(lane, 2)},
            device_id_type=MESH,
        )

    def back_copy(other):
        return pltpu.make_async_remote_copy(
            src_ref=back_src.at[other],
            dst_ref=cons_all.at[pol, me],
            send_sem=misc.at[4],
            recv_sem=back_recv.at[me // plane],
            device_id={"freq": other},
            device_id_type=MESH,
        )

    def swap_copy(base):
        view = cons_all.at[pol, pl.ds(base, plane)]
        return pltpu.make_async_remote_copy(
            src_ref=view,
            dst_ref=view,
            send_sem=misc.at[5],
            recv_sem=misc.at[6],
            device_id={"bl": group - 1 - lane},
            device_id_type=MESH,
        )

    fwd_all[me] = fwd_src[me]
    wait_bytes(fwd_all, freqs - 1, misc.at[1])
    for odd in range(2):

        @pl.when(chan == odd)
        def _():
            acc = [None] * 4
            for f in range(freqs):
                value = fwd_all[f]
                for m in range(4):
                    term = value * float(basis[2 * f + odd, m])
                    acc[m] = term if acc[m] is None else acc[m] + term
            for m in range(4):
                part_src[m] = acc[m]

    part_copy().start()
    part_copy().wait_recv()
    whole = [part_src[m] + part_in[m] for m in range(4)]
    forward = []
    for row in range(4):
        acc = whole[row]
        for col in range(row):
            acc = acc - float(factor[row, col]) * forward[col]
        forward.append(acc * float(1.0 / factor[row, row]))
    coeffs = [None] * 4
    for row in range(3, -1, -1):
        acc = forward[row]
        for col in range(row + 1, 4):
            acc = acc - float(factor[col, row]) * coeffs[col]
        coeffs[row] = acc * float(1.0 / factor[row, row])
    for f in range(freqs):
        for odd in range(2):
            value = coeffs[0] * float(basis[2 * f + odd, 0])
            for m in range(1, 4):
                value = value + coeffs[m] * float(basis[2 * f + odd, m])
            back_src[f, odd] = value
    far_first(lambda other: back_copy(other).start())
    cons_all[pol, me] = back_src[me]

    def tiles(take):
        for part in range(2):
            for odd in range(2):
                for n in range(stations):
                    take(part, odd, n, n // per_owner, part * per_owner + n % per_owner)

    for slot in range(1, group):
        gain_copy(slot, OFFSETS[slot]).wait_recv()

    def emit_gains(part, odd, n, owner, row):
        at = part * HALF + n
        tile = jnp.concatenate([gains_all[odd, at : at + 1, 0:dirs], gains_all[2 + odd, at : at + 1, 0:dirs]], axis=0)
        gains_out[part, odd, n] = tile
        dual_out[part, odd, n] = dual_in[part, odd, n] + tile

    tiles(emit_gains)

    here = me // plane
    for ahead in sorted(range(planes), key=lambda d: min(d, planes - d)):
        from_plane = lax.rem(here + ahead, planes)
        count = plane if ahead else plane - 1
        view = cons_all.at[pol, pl.ds(from_plane * plane, count)]
        pltpu.make_async_copy(view, view, back_recv.at[from_plane]).wait()
        swap_copy(from_plane * plane).start()
    wait_bytes(cons_all.at[1 - pol], freqs, misc.at[6])

    def emit_cons(part, odd, n, owner, row):
        tile = jnp.concatenate(
            [cons_all[0, owner, odd, row : row + 1, 0:dirs], cons_all[1, owner, odd, row : row + 1, 0:dirs]], axis=0
        )
        cons_out[part, odd, n] = tile
        dual_out[part, odd, n] = dual_out[part, odd, n] - tile

    tiles(emit_cons)

    for slot in range(1, group):
        coh_copy(slot, OFFSETS[slot]).wait_send()
        aux_copy(slot, OFFSETS[slot]).wait_send()
        gain_copy(slot, OFFSETS[slot]).wait_send()
    wait_bytes(fwd_src, freqs - 1, misc.at[0])
    part_copy().wait_send()
    wait_bytes(back_src, freqs - 1, misc.at[4])
    wait_bytes(cons_all.at[pol], freqs, misc.at[5])


def solution(mesh):
    freqs = mesh.shape["freq"]

    def step(vis, coh, pairs, flags, gains_in, cons_in, dual_in, penalty, damping):
        dirs = gains_in.shape[-2]
        rows = coh.shape[-1]
        ktiles = -(-dirs // 8)
        krows = 8 * ktiles
        term_rows = 32 * ktiles + 16 * (-(-ktiles // 2))
        group = len(OFFSETS)
        per_owner = HALF // freqs
        planes = freqs // min(8, freqs)
        lanes = 2 * HALF
        f32, b16 = jnp.float32, jnp.bfloat16
        whole = pl.BlockSpec(memory_space=pltpu.VMEM)
        scratch = [
            pltpu.VMEM((group - 1, 2 * dirs, rows), f32),
            pltpu.VMEM((group, 2 * dirs, rows), f32),
            pltpu.VMEM((group - 1, 4, rows), f32),
            pltpu.VMEM((group, 4, rows), f32),
            pltpu.VMEM((group, lanes, 2 * rows), b16),
            pltpu.VMEM((group, 2 * rows, lanes), b16),
            pltpu.VMEM((group, 2 * krows, 2 * rows), f32),
            pltpu.VMEM((group, term_rows, 2 * rows), b16),
            pltpu.VMEM((term_rows, lanes), f32),
            pltpu.VMEM((krows, lanes), f32),
            pltpu.VMEM((krows, lanes), f32),
            pltpu.VMEM((lanes, lanes), f32),
            pltpu.VMEM((krows, lanes), f32),
            pltpu.VMEM((2 * krows, lanes), b16),
            pltpu.VMEM((lanes, lanes), f32),
            pltpu.VMEM((group, lanes, lanes), f32),
            pltpu.VMEM((freqs, 2 * per_owner, lanes), f32),
            pltpu.VMEM((freqs, 2 * per_owner, lanes), f32),
            pltpu.VMEM((4, 2 * per_owner, lanes), f32),
            pltpu.VMEM((4, 2 * per_owner, lanes), f32),
            pltpu.VMEM((freqs, 2, 2 * per_owner, lanes), f32),
            pltpu.VMEM((2, freqs, 2, 2 * per_owner, lanes), f32),
        ] + [pltpu.SemaphoreType.DMA((n,)) for n in (group,) * 6 + (planes, 8)]

        def turn(value):
            return jnp.transpose(value, (0, 1, 4, 2, 3))

        gains_in, cons_in, dual_in = turn(gains_in), turn(cons_in), turn(dual_in)
        out = jax.ShapeDtypeStruct(gains_in.shape, f32)
        outs = pl.pallas_call(
            functools.partial(kernel, freqs),
            out_shape=(out, out, out),
            in_specs=[whole] * 8 + [pl.BlockSpec(memory_space=pltpu.SMEM)],
            out_specs=(whole, whole, whole),
            scratch_shapes=scratch,
            compiler_params=pltpu.CompilerParams(
                collective_id=0, has_side_effects=True, vmem_limit_bytes=40 * 1024 * 1024
            ),
        )(vis, coh, pairs, flags, gains_in, cons_in, dual_in, penalty.reshape(1, dirs), damping)
        return tuple(jnp.transpose(value, (0, 1, 3, 4, 2)) for value in outs)

    spread = P(None, "freq", None, None, None)
    return jax.shard_map(
        step,
        mesh=mesh,
        in_specs=(
            P(None, "freq", None, "bl"),
            P(None, "freq", None, None, "bl"),
            P(None, "bl"),
            P("freq", "bl"),
            spread,
            spread,
            spread,
            P(),
            P(),
        ),
        out_specs=(spread, spread, spread),
        check_vma=False,
    )
```

```python
import functools

import jax
import jax.numpy as jnp
import numpy as np
from jax import lax
from jax.experimental import pallas as pl
from jax.experimental.pallas import tpu as pltpu
from jax.sharding import PartitionSpec as P

MESH = pl.DeviceIdType.MESH
OFFSETS = (0, 1, 3, 2)
HALF = 64
WIDE = 256


def bernstein(position):
    other = 1.0 - position
    return np.stack(
        [
            other * other * other,
            3.0 * position * other * other,
            3.0 * position * position * other,
            position * position * position,
        ],
        axis=-1,
    )


def kernel(
    freqs,
    vis,
    coh,
    pairs,
    flags,
    gains_in,
    cons_in,
    dual_in,
    penalty,
    damping,
    gains_out,
    cons_out,
    dual_out,
    send_coh,
    coh_all,
    send_aux,
    aux_all,
    hot,
    hot_t,
    picked,
    terms,
    sums,
    gains,
    target,
    dual,
    rate,
    table,
    pad,
    gains_all,
    fwd_src,
    fwd_all,
    part_src,
    part_in,
    back_src,
    cons_all,
    coh_send,
    coh_recv,
    aux_send,
    aux_recv,
    gain_send,
    gain_recv,
    back_recv,
    misc,
    rounds,
):
    stations, dirs = gains_in.shape[2], gains_in.shape[4]
    rows = coh.shape[-1]
    ktiles = gains.shape[0] // 8
    per_owner = HALF // freqs
    plane = min(8, freqs)
    planes = freqs // plane
    even = dirs // 8 * 8
    rest = dirs - even
    me = lax.axis_index("freq")
    lane = lax.axis_index("bl")
    group = len(OFFSETS)

    def place(problem):
        return lax.rem(problem, 2), problem // 2

    deep = max(1, freqs // 8)
    wide = freqs // (2 * deep)

    def freq_at(dz, dy, dc):
        z = lax.rem(me // (2 * wide) + dz, deep)
        y = lax.rem(me // 2 % wide + dy, wide)
        return (z * wide + y) * 2 + lax.rem(me % 2 + dc, 2)

    near = sorted({d % deep for d in (1, 2, -1, -2)} - {0})
    round_z = [freq_at(d, 0, 0) for d in sorted({2 % deep, -2 % deep} - {0})]
    round_y = [freq_at(0, d, 0) for d in range(1, wide)]
    round_core = [freq_at(0, 0, 1)]
    greeted = [freq_at(d, 0, 0) for d in near] + round_y + round_core
    barrier = pltpu.get_barrier_semaphore()
    for off in OFFSETS[1:]:
        other = lax.rem(lane + off, group)
        pl.semaphore_signal(barrier, inc=1, device_id={"bl": other}, device_id_type=MESH)
    for other in greeted:
        pl.semaphore_signal(barrier, inc=1, device_id={"freq": other}, device_id_type=MESH)

    def tell(stage, others):
        for other in others:
            pl.semaphore_signal(rounds.at[stage], inc=1, device_id={"freq": other}, device_id_type=MESH)

    def hear(stage, others):
        if others:
            pl.semaphore_wait(rounds.at[stage], len(others))

    def fill(off, coh_to, aux_to):
        chan, pol = place(lax.rem(lane + off, group))
        weight = flags[pl.ds(chan, 1), :].astype(jnp.float32)
        for part in range(2):
            value = coh[part, chan, pol].astype(jnp.float32) * weight
            coh_to[part * even : (part + 1) * even, :] = value[0:even]
            coh_to[2 * even + part * rest : 2 * even + (part + 1) * rest, :] = value[even:dirs]
            aux_to[part : part + 1, :] = vis[part, chan, pl.ds(pol, 1), :] * weight
            aux_to[2 + part : 3 + part, :] = pairs[part : part + 1, :].astype(jnp.float32)

    def coh_copy(slot, off):
        return pltpu.make_async_remote_copy(
            src_ref=send_coh.at[slot - 1],
            dst_ref=coh_all.at[slot],
            send_sem=coh_send.at[slot],
            recv_sem=coh_recv.at[slot],
            device_id={"bl": lax.rem(lane + off, group)},
            device_id_type=MESH,
        )

    def aux_copy(slot, off):
        return pltpu.make_async_remote_copy(
            src_ref=send_aux.at[slot - 1],
            dst_ref=aux_all.at[slot],
            send_sem=aux_send.at[slot],
            recv_sem=aux_recv.at[slot],
            device_id={"bl": lax.rem(lane + off, group)},
            device_id_type=MESH,
        )

    for slot in range(1, group):
        fill(OFFSETS[slot], send_coh.at[slot - 1], send_aux.at[slot - 1])
    pl.semaphore_wait(barrier, group - 1 + len(greeted))
    for slot in range(1, group):
        aux_copy(slot, OFFSETS[slot]).start()
    for slot in range(1, group):
        coh_copy(slot, OFFSETS[slot]).start()
    tell(0, round_z)
    fill(0, coh_all.at[0], aux_all.at[0])

    lanes = lax.broadcasted_iota(jnp.int32, (8 * ktiles, 2 * HALF), 1)
    low = lanes < HALF
    chan, pol = place(lane)

    def pack(ref, to):
        to[...] = jnp.zeros_like(to)
        for part in range(2):
            for n in range(stations):
                to[part * HALF + n : part * HALF + n + 1, 0:dirs] = ref[part, chan, n, pl.ds(pol, 1), :]

    pack(gains_in, pad)
    gains[...] = pad[...].T[0 : 8 * ktiles, :]
    pack(dual_in, dual)
    pack(cons_in, pad)
    target[...] = (pad[...] - dual[...]).T[0 : 8 * ktiles, :]
    pad[...] = jnp.zeros_like(pad)
    pad[0:1, 0:dirs] = penalty[...]
    rate[...] = jnp.broadcast_to(pad[0:1, :], (2 * HALF, 2 * HALF)).T[0 : 8 * ktiles, :]

    def hots(slot):
        ids = lax.broadcasted_iota(jnp.int32, (2 * HALF, rows), 0)
        ids = jnp.where(ids >= HALF, ids - HALF, ids).astype(jnp.float32)
        for part in range(2):
            ones = jnp.where(ids == aux_all[slot, 2 + part : 3 + part, :], 1.0, 0.0)
            hot[slot, :, part * rows : (part + 1) * rows] = ones.astype(jnp.bfloat16)
            hot_t[slot, part * rows : (part + 1) * rows, :] = ones.T.astype(jnp.bfloat16)

    def spread_table():
        value = gains[...]
        high = value.astype(jnp.bfloat16).astype(jnp.float32)
        rest = value - high
        real = jnp.where(low, high, pltpu.roll(rest, HALF, 1))
        imag = jnp.where(low, pltpu.roll(high, HALF, 1), rest)
        for k in range(ktiles):
            both = jnp.concatenate([real[8 * k : 8 * k + 8], imag[8 * k : 8 * k + 8]], axis=0)
            table[16 * k : 16 * k + 16, :] = both.astype(jnp.bfloat16)

    def gather(slot):
        picked[slot] = jnp.dot(table[...], hot[slot], preferred_element_type=jnp.float32)

    def vector(slot):
        for at in range(0, rows, WIDE):
            first = slice(at, at + WIDE)
            second = slice(rows + at, rows + at + WIDE)

            def load(k):
                if 8 * k < even:
                    cre = coh_all[slot, 8 * k : 8 * k + 8, first]
                    cim = coh_all[slot, even + 8 * k : even + 8 * k + 8, first]
                else:
                    cre = coh_all[slot, 2 * even : 2 * even + 8, first]
                    cim = pltpu.roll(cre, rest, 0)
                pre = picked[slot, 16 * k : 16 * k + 8, first]
                pim = picked[slot, 16 * k + 8 : 16 * k + 16, first]
                qre = picked[slot, 16 * k : 16 * k + 8, second]
                qim = picked[slot, 16 * k + 8 : 16 * k + 16, second]
                return cre, cim, pre, pim, qre, qim

            mre = jnp.zeros((8, WIDE), jnp.float32)
            mim = jnp.zeros((8, WIDE), jnp.float32)
            for k in range(ktiles):
                cre, cim, pre, pim, qre, qim = load(k)
                tre = cre * qre + cim * qim
                tim = cim * qre - cre * qim
                mre = mre + (pre * tre - pim * tim)
                mim = mim + (pre * tim + pim * tre)
            rre = aux_all[slot, 0:1, first] - jnp.sum(mre, axis=0, keepdims=True)
            rim = aux_all[slot, 1:2, first] - jnp.sum(mim, axis=0, keepdims=True)
            rre = jnp.broadcast_to(rre, (8, WIDE))
            rim = jnp.broadcast_to(rim, (8, WIDE))
            held = [None, None]
            for k in range(ktiles):
                cre, cim, pre, pim, qre, qim = load(k)
                are = rre * cre + rim * cim
                aim = rim * cre - rre * cim
                square = cre * cre + cim * cim
                sides = (
                    (first, are * qre - aim * qim, are * qim + aim * qre, square * (qre * qre + qim * qim)),
                    (second, are * pre + aim * pim, are * pim - aim * pre, square * (pre * pre + pim * pim)),
                )
                for side, (cols, real, imag, curv) in enumerate(sides):
                    both = jnp.concatenate([real, imag], axis=0)
                    high = both.astype(jnp.bfloat16)
                    terms[slot, 32 * k : 32 * k + 16, cols] = high
                    terms[slot, 32 * k + 16 : 32 * k + 32, cols] = (both - high.astype(jnp.float32)).astype(jnp.bfloat16)
                    base = 32 * ktiles + 8 * (k - k % 2)
                    if k % 2:
                        both = jnp.concatenate([held[side], curv], axis=0)
                        terms[slot, base : base + 16, cols] = both.astype(jnp.bfloat16)
                    elif k == ktiles - 1:
                        both = jnp.concatenate([curv, jnp.zeros_like(curv)], axis=0)
                        terms[slot, base : base + 16, cols] = both.astype(jnp.bfloat16)
                    held[side] = curv

    def scatter(slot):
        sums[...] += jnp.dot(terms[slot], hot_t[slot], preferred_element_type=jnp.float32)

    def update(damp):
        half = lax.broadcasted_iota(jnp.int32, (8, 2 * HALF), 1) < HALF
        for k in range(ktiles):
            at = slice(8 * k, 8 * k + 8)
            real = sums[32 * k : 32 * k + 8, :] + sums[32 * k + 16 : 32 * k + 24, :]
            imag = sums[32 * k + 8 : 32 * k + 16, :] + sums[32 * k + 24 : 32 * k + 32, :]
            numer = jnp.where(half, real, imag)
            curv = sums[32 * ktiles + 8 * k : 32 * ktiles + 8 * k + 8, :]
            value = gains[at, :]
            pull = rate[at, :]
            gains[at, :] = value + (numer - pull * (value - target[at, :])) / (curv + damp + pull)

    def one_step(step, carry):
        spread_table()
        sums[...] = jnp.zeros_like(sums)
        for slot in range(group):
            gather(slot)
        for slot in range(group):
            vector(slot)
            scatter(slot)
        update(damping[step])
        return carry

    spread_table()
    sums[...] = jnp.zeros_like(sums)
    for slot in range(group):
        if slot:
            aux_copy(slot, 0).wait_recv()
        hots(slot)
        gather(slot)
        if slot:
            coh_copy(slot, 0).wait_recv()
        vector(slot)
        scatter(slot)
        if slot == 0:
            hear(0, round_z)
            tell(1, round_y)
        elif slot == 1:
            hear(1, round_y)
            tell(2, round_core)
        elif slot == 2:
            hear(2, round_core)
    update(damping[0])
    lax.fori_loop(1, damping.shape[0], one_step, 0)

    pad[0 : 8 * ktiles, :] = gains[...]
    pad[8 * ktiles : 2 * HALF, :] = jnp.zeros((2 * HALF - 8 * ktiles, 2 * HALF), jnp.float32)
    solved = pad[...].T
    gains_all[lane] = solved
    blend = solved + dual[...]
    for owner in range(freqs):
        for part in range(2):
            base = part * HALF + owner * per_owner
            fwd_src[owner, part * per_owner : (part + 1) * per_owner, :] = blend[base : base + per_owner, :]

    def far_first(send):
        here = me // plane
        order = sorted(range(planes), key=lambda d: -min(d, planes - d))
        for ahead in order:
            base = lax.rem(here + ahead, planes) * plane

            def one(step, carry):
                send(base + lax.rem(me + step, plane))
                return carry

            lax.fori_loop(0 if ahead else 1, plane, one, 0)

    def fwd_copy(other):
        return pltpu.make_async_remote_copy(
            src_ref=fwd_src.at[other],
            dst_ref=fwd_all.at[me],
            send_sem=misc.at[0],
            recv_sem=misc.at[1],
            device_id={"freq": other},
            device_id_type=MESH,
        )

    far_first(lambda other: fwd_copy(other).start())

    def gain_copy(slot, off):
        return pltpu.make_async_remote_copy(
            src_ref=gains_all.at[lane],
            dst_ref=gains_all.at[lane],
            send_sem=gain_send.at[slot],
            recv_sem=gain_recv.at[slot],
            device_id={"bl": lax.rem(lane + off, group)},
            device_id_type=MESH,
        )

    for slot in range(1, group):
        gain_copy(slot, OFFSETS[slot]).start()

    def wait_bytes(ref, count, sem):
        view = ref.at[0:count]
        pltpu.make_async_copy(view, view, sem).wait()

    total = 2 * freqs
    basis = bernstein((np.arange(total) + 0.5) / total)
    factor = np.linalg.cholesky(basis.T @ basis)

    def part_copy():
        return pltpu.make_async_remote_copy(
            src_ref=part_src,
            dst_ref=part_in,
            send_sem=misc.at[2],
            recv_sem=misc.at[3],
            device_id={"bl": lane + 1 - 2 * lax.rem(lane, 2)},
            device_id_type=MESH,
        )

    def back_copy(other):
        return pltpu.make_async_remote_copy(
            src_ref=back_src.at[other],
            dst_ref=cons_all.at[pol, me],
            send_sem=misc.at[4],
            recv_sem=back_recv.at[me // plane],
            device_id={"freq": other},
            device_id_type=MESH,
        )

    def swap_copy(base):
        view = cons_all.at[pol, pl.ds(base, plane)]
        return pltpu.make_async_remote_copy(
            src_ref=view,
            dst_ref=view,
            send_sem=misc.at[5],
            recv_sem=misc.at[6],
            device_id={"bl": group - 1 - lane},
            device_id_type=MESH,
        )

    fwd_all[me] = fwd_src[me]
    wait_bytes(fwd_all, freqs - 1, misc.at[1])
    for odd in range(2):

        @pl.when(chan == odd)
        def _():
            acc = [None] * 4
            for f in range(freqs):
                value = fwd_all[f]
                for m in range(4):
                    term = value * float(basis[2 * f + odd, m])
                    acc[m] = term if acc[m] is None else acc[m] + term
            for m in range(4):
                part_src[m] = acc[m]

    part_copy().start()
    part_copy().wait_recv()
    whole = [part_src[m] + part_in[m] for m in range(4)]
    forward = []
    for row in range(4):
        acc = whole[row]
        for col in range(row):
            acc = acc - float(factor[row, col]) * forward[col]
        forward.append(acc * float(1.0 / factor[row, row]))
    coeffs = [None] * 4
    for row in range(3, -1, -1):
        acc = forward[row]
        for col in range(row + 1, 4):
            acc = acc - float(factor[col, row]) * coeffs[col]
        coeffs[row] = acc * float(1.0 / factor[row, row])
    for f in range(freqs):
        for odd in range(2):
            value = coeffs[0] * float(basis[2 * f + odd, 0])
            for m in range(1, 4):
                value = value + coeffs[m] * float(basis[2 * f + odd, m])
            back_src[f, odd] = value
    far_first(lambda other: back_copy(other).start())
    cons_all[pol, me] = back_src[me]

    def tiles(take):
        for part in range(2):
            for odd in range(2):
                for n in range(stations):
                    take(part, odd, n, n // per_owner, part * per_owner + n % per_owner)

    for slot in range(1, group):
        gain_copy(slot, OFFSETS[slot]).wait_recv()

    def emit_gains(part, odd, n, owner, row):
        at = part * HALF + n
        tile = jnp.concatenate([gains_all[odd, at : at + 1, 0:dirs], gains_all[2 + odd, at : at + 1, 0:dirs]], axis=0)
        gains_out[part, odd, n] = tile
        dual_out[part, odd, n] = dual_in[part, odd, n] + tile

    tiles(emit_gains)

    here = me // plane
    for ahead in sorted(range(planes), key=lambda d: min(d, planes - d)):
        from_plane = lax.rem(here + ahead, planes)
        count = plane if ahead else plane - 1
        view = cons_all.at[pol, pl.ds(from_plane * plane, count)]
        pltpu.make_async_copy(view, view, back_recv.at[from_plane]).wait()
        swap_copy(from_plane * plane).start()
    wait_bytes(cons_all.at[1 - pol], freqs, misc.at[6])

    def emit_cons(part, odd, n, owner, row):
        tile = jnp.concatenate(
            [cons_all[0, owner, odd, row : row + 1, 0:dirs], cons_all[1, owner, odd, row : row + 1, 0:dirs]], axis=0
        )
        cons_out[part, odd, n] = tile
        dual_out[part, odd, n] = dual_out[part, odd, n] - tile

    tiles(emit_cons)

    for slot in range(1, group):
        coh_copy(slot, OFFSETS[slot]).wait_send()
        aux_copy(slot, OFFSETS[slot]).wait_send()
        gain_copy(slot, OFFSETS[slot]).wait_send()
    wait_bytes(fwd_src, freqs - 1, misc.at[0])
    part_copy().wait_send()
    wait_bytes(back_src, freqs - 1, misc.at[4])
    wait_bytes(cons_all.at[pol], freqs, misc.at[5])


def solution(mesh):
    freqs = mesh.shape["freq"]

    def step(vis, coh, pairs, flags, gains_in, cons_in, dual_in, penalty, damping):
        dirs = gains_in.shape[-2]
        rows = coh.shape[-1]
        ktiles = -(-dirs // 8)
        krows = 8 * ktiles
        term_rows = 32 * ktiles + 16 * (-(-ktiles // 2))
        group = len(OFFSETS)
        per_owner = HALF // freqs
        planes = freqs // min(8, freqs)
        lanes = 2 * HALF
        f32, b16 = jnp.float32, jnp.bfloat16
        whole = pl.BlockSpec(memory_space=pltpu.VMEM)
        scratch = [
            pltpu.VMEM((group - 1, 2 * dirs, rows), f32),
            pltpu.VMEM((group, 2 * dirs, rows), f32),
            pltpu.VMEM((group - 1, 4, rows), f32),
            pltpu.VMEM((group, 4, rows), f32),
            pltpu.VMEM((group, lanes, 2 * rows), b16),
            pltpu.VMEM((group, 2 * rows, lanes), b16),
            pltpu.VMEM((group, 2 * krows, 2 * rows), f32),
            pltpu.VMEM((group, term_rows, 2 * rows), b16),
            pltpu.VMEM((term_rows, lanes), f32),
            pltpu.VMEM((krows, lanes), f32),
            pltpu.VMEM((krows, lanes), f32),
            pltpu.VMEM((lanes, lanes), f32),
            pltpu.VMEM((krows, lanes), f32),
            pltpu.VMEM((2 * krows, lanes), b16),
            pltpu.VMEM((lanes, lanes), f32),
            pltpu.VMEM((group, lanes, lanes), f32),
            pltpu.VMEM((freqs, 2 * per_owner, lanes), f32),
            pltpu.VMEM((freqs, 2 * per_owner, lanes), f32),
            pltpu.VMEM((4, 2 * per_owner, lanes), f32),
            pltpu.VMEM((4, 2 * per_owner, lanes), f32),
            pltpu.VMEM((freqs, 2, 2 * per_owner, lanes), f32),
            pltpu.VMEM((2, freqs, 2, 2 * per_owner, lanes), f32),
        ] + [pltpu.SemaphoreType.DMA((n,)) for n in (group,) * 6 + (planes, 8)]
        scratch.append(pltpu.SemaphoreType.REGULAR((3,)))

        def turn(value):
            return jnp.transpose(value, (0, 1, 4, 2, 3))

        gains_in, cons_in, dual_in = turn(gains_in), turn(cons_in), turn(dual_in)
        out = jax.ShapeDtypeStruct(gains_in.shape, f32)
        outs = pl.pallas_call(
            functools.partial(kernel, freqs),
            out_shape=(out, out, out),
            in_specs=[whole] * 8 + [pl.BlockSpec(memory_space=pltpu.SMEM)],
            out_specs=(whole, whole, whole),
            scratch_shapes=scratch,
            compiler_params=pltpu.CompilerParams(
                collective_id=0, has_side_effects=True, vmem_limit_bytes=40 * 1024 * 1024
            ),
        )(vis, coh, pairs, flags, gains_in, cons_in, dual_in, penalty.reshape(1, dirs), damping)
        return tuple(jnp.transpose(value, (0, 1, 3, 4, 2)) for value in outs)

    spread = P(None, "freq", None, None, None)
    return jax.shard_map(
        step,
        mesh=mesh,
        in_specs=(
            P(None, "freq", None, "bl"),
            P(None, "freq", None, None, "bl"),
            P(None, "bl"),
            P("freq", "bl"),
            spread,
            spread,
            spread,
            P(),
            P(),
        ),
        out_specs=(spread, spread, spread),
        check_vma=False,
    )
```

```python
import functools

import jax
import jax.numpy as jnp
import numpy as np
from jax import lax
from jax.experimental import pallas as pl
from jax.experimental.pallas import tpu as pltpu
from jax.sharding import PartitionSpec as P

MESH = pl.DeviceIdType.MESH
OFFSETS = (0, 1, 3, 2)
HALF = 64
WIDE = 256


def bernstein(position):
    other = 1.0 - position
    return np.stack(
        [
            other * other * other,
            3.0 * position * other * other,
            3.0 * position * position * other,
            position * position * position,
        ],
        axis=-1,
    )


def kernel(
    freqs,
    vis,
    coh,
    pairs,
    flags,
    gains_in,
    cons_in,
    dual_in,
    penalty,
    damping,
    gains_out,
    cons_out,
    send_coh,
    coh_all,
    send_aux,
    aux_all,
    hot,
    hot_t,
    picked,
    terms,
    sums,
    gains,
    target,
    dual,
    rate,
    table,
    pad,
    gains_all,
    fwd_src,
    fwd_all,
    back_src,
    cons_all,
    coh_send,
    coh_recv,
    aux_send,
    aux_recv,
    gain_send,
    gain_recv,
    cons_send,
    cons_recv,
    back_recv,
    misc,
    rounds,
):
    stations, dirs = gains_in.shape[2], gains_in.shape[4]
    rows = coh.shape[-1]
    ktiles = gains.shape[0] // 8
    per_owner = HALF // freqs
    plane = min(8, freqs)
    planes = freqs // plane
    even = dirs // 8 * 8
    rest = dirs - even
    me = lax.axis_index("freq")
    lane = lax.axis_index("bl")
    group = len(OFFSETS)

    def place(problem):
        return lax.rem(problem, 2), problem // 2

    deep = max(1, freqs // 8)
    wide = freqs // (2 * deep)

    def freq_at(dz, dy, dc):
        z = lax.rem(me // (2 * wide) + dz, deep)
        y = lax.rem(me // 2 % wide + dy, wide)
        return (z * wide + y) * 2 + lax.rem(me % 2 + dc, 2)

    near = sorted({d % deep for d in (1, 2, -1, -2)} - {0})
    round_z = [freq_at(d, 0, 0) for d in sorted({2 % deep, -2 % deep} - {0})]
    round_y = [freq_at(0, d, 0) for d in range(1, wide)]
    round_core = [freq_at(0, 0, 1)]
    greeted = [freq_at(d, 0, 0) for d in near] + round_y + round_core
    barrier = pltpu.get_barrier_semaphore()
    for off in OFFSETS[1:]:
        other = lax.rem(lane + off, group)
        pl.semaphore_signal(barrier, inc=1, device_id={"bl": other}, device_id_type=MESH)
    for other in greeted:
        pl.semaphore_signal(barrier, inc=1, device_id={"freq": other}, device_id_type=MESH)

    def tell(stage, others):
        for other in others:
            pl.semaphore_signal(rounds.at[stage], inc=1, device_id={"freq": other}, device_id_type=MESH)

    def hear(stage, others):
        if others:
            pl.semaphore_wait(rounds.at[stage], len(others))

    def fill(off, coh_to, aux_to):
        chan, pol = place(lax.rem(lane + off, group))
        weight = flags[pl.ds(chan, 1), :].astype(jnp.float32)
        for part in range(2):
            value = coh[part, chan, pol].astype(jnp.float32) * weight
            coh_to[part * even : (part + 1) * even, :] = value[0:even]
            coh_to[2 * even + part * rest : 2 * even + (part + 1) * rest, :] = value[even:dirs]
            aux_to[part : part + 1, :] = vis[part, chan, pl.ds(pol, 1), :] * weight
            aux_to[2 + part : 3 + part, :] = pairs[part : part + 1, :].astype(jnp.float32)

    def coh_copy(slot, off):
        return pltpu.make_async_remote_copy(
            src_ref=send_coh.at[slot - 1],
            dst_ref=coh_all.at[slot],
            send_sem=coh_send.at[slot],
            recv_sem=coh_recv.at[slot],
            device_id={"bl": lax.rem(lane + off, group)},
            device_id_type=MESH,
        )

    def aux_copy(slot, off):
        return pltpu.make_async_remote_copy(
            src_ref=send_aux.at[slot - 1],
            dst_ref=aux_all.at[slot],
            send_sem=aux_send.at[slot],
            recv_sem=aux_recv.at[slot],
            device_id={"bl": lax.rem(lane + off, group)},
            device_id_type=MESH,
        )

    for slot in range(1, group):
        fill(OFFSETS[slot], send_coh.at[slot - 1], send_aux.at[slot - 1])
    pl.semaphore_wait(barrier, group - 1 + len(greeted))
    for slot in range(1, group):
        aux_copy(slot, OFFSETS[slot]).start()
    for slot in range(1, group):
        coh_copy(slot, OFFSETS[slot]).start()
    tell(0, round_z)
    fill(0, coh_all.at[0], aux_all.at[0])

    lanes = lax.broadcasted_iota(jnp.int32, (8 * ktiles, 2 * HALF), 1)
    low = lanes < HALF
    chan, pol = place(lane)
    mate = lane + 1 - 2 * chan

    def pack(ref, to):
        to[...] = jnp.zeros_like(to)
        for part in range(2):
            for n in range(stations):
                to[part * HALF + n : part * HALF + n + 1, 0:dirs] = ref[part, chan, n, pl.ds(pol, 1), :]

    pack(gains_in, pad)
    gains[...] = pad[...].T[0 : 8 * ktiles, :]
    pack(dual_in, dual)
    pack(cons_in, pad)
    target[...] = (pad[...] - dual[...]).T[0 : 8 * ktiles, :]
    pad[...] = jnp.zeros_like(pad)
    pad[0:1, 0:dirs] = penalty[...]
    rate[...] = jnp.broadcast_to(pad[0:1, :], (2 * HALF, 2 * HALF)).T[0 : 8 * ktiles, :]

    def hots(slot):
        ids = lax.broadcasted_iota(jnp.int32, (2 * HALF, rows), 0)
        ids = jnp.where(ids >= HALF, ids - HALF, ids).astype(jnp.float32)
        for part in range(2):
            ones = jnp.where(ids == aux_all[slot, 2 + part : 3 + part, :], 1.0, 0.0)
            at = slice((2 * slot + part) * rows, (2 * slot + part + 1) * rows)
            hot[:, at] = ones.astype(jnp.bfloat16)
            hot_t[at, :] = ones.T.astype(jnp.bfloat16)

    def spread_table():
        value = gains[...]
        high = value.astype(jnp.bfloat16).astype(jnp.float32)
        rest = value - high
        real = jnp.where(low, high, pltpu.roll(rest, HALF, 1))
        imag = jnp.where(low, pltpu.roll(high, HALF, 1), rest)
        for k in range(ktiles):
            both = jnp.concatenate([real[8 * k : 8 * k + 8], imag[8 * k : 8 * k + 8]], axis=0)
            table[16 * k : 16 * k + 16, :] = both.astype(jnp.bfloat16)

    def gather(slot, count=1):
        at = slice(2 * slot * rows, 2 * (slot + count) * rows)
        picked[:, at] = jnp.dot(table[...], hot[:, at], preferred_element_type=jnp.float32)

    def vector(slot):
        for at in range(0, rows, WIDE):
            sample = slice(at, at + WIDE)
            first = slice(2 * slot * rows + at, 2 * slot * rows + at + WIDE)
            second = slice((2 * slot + 1) * rows + at, (2 * slot + 1) * rows + at + WIDE)

            def load(k):
                if 8 * k < even:
                    cre = coh_all[slot, 8 * k : 8 * k + 8, sample]
                    cim = coh_all[slot, even + 8 * k : even + 8 * k + 8, sample]
                else:
                    cre = coh_all[slot, 2 * even : 2 * even + 8, sample]
                    cim = pltpu.roll(cre, rest, 0)
                pre = picked[16 * k : 16 * k + 8, first]
                pim = picked[16 * k + 8 : 16 * k + 16, first]
                qre = picked[16 * k : 16 * k + 8, second]
                qim = picked[16 * k + 8 : 16 * k + 16, second]
                return cre, cim, pre, pim, qre, qim

            mre = jnp.zeros((8, WIDE), jnp.float32)
            mim = jnp.zeros((8, WIDE), jnp.float32)
            for k in range(ktiles):
                cre, cim, pre, pim, qre, qim = load(k)
                tre = cre * qre + cim * qim
                tim = cim * qre - cre * qim
                mre = mre + (pre * tre - pim * tim)
                mim = mim + (pre * tim + pim * tre)
            rre = aux_all[slot, 0:1, sample] - jnp.sum(mre, axis=0, keepdims=True)
            rim = aux_all[slot, 1:2, sample] - jnp.sum(mim, axis=0, keepdims=True)
            rre = jnp.broadcast_to(rre, (8, WIDE))
            rim = jnp.broadcast_to(rim, (8, WIDE))
            held = [None, None]
            for k in range(ktiles):
                cre, cim, pre, pim, qre, qim = load(k)
                are = rre * cre + rim * cim
                aim = rim * cre - rre * cim
                square = cre * cre + cim * cim
                sides = (
                    (first, are * qre - aim * qim, are * qim + aim * qre, square * (qre * qre + qim * qim)),
                    (second, are * pre + aim * pim, are * pim - aim * pre, square * (pre * pre + pim * pim)),
                )
                for side, (cols, real, imag, curv) in enumerate(sides):
                    both = jnp.concatenate([real, imag], axis=0)
                    high = both.astype(jnp.bfloat16)
                    terms[32 * k : 32 * k + 16, cols] = high
                    terms[32 * k + 16 : 32 * k + 32, cols] = (both - high.astype(jnp.float32)).astype(jnp.bfloat16)
                    base = 32 * ktiles + 8 * (k - k % 2)
                    if k % 2:
                        both = jnp.concatenate([held[side], curv], axis=0)
                        terms[base : base + 16, cols] = both.astype(jnp.bfloat16)
                    elif k == ktiles - 1:
                        both = jnp.concatenate([curv, jnp.zeros_like(curv)], axis=0)
                        terms[base : base + 16, cols] = both.astype(jnp.bfloat16)
                    held[side] = curv

    def scatter(slot, count=1):
        at = slice(2 * slot * rows, 2 * (slot + count) * rows)
        value = jnp.dot(terms[:, at], hot_t[at, :], preferred_element_type=jnp.float32)
        sums[...] = value if slot == 0 else sums[...] + value

    def update(damp):
        half = lax.broadcasted_iota(jnp.int32, (8, 2 * HALF), 1) < HALF
        for k in range(ktiles):
            at = slice(8 * k, 8 * k + 8)
            real = sums[32 * k : 32 * k + 8, :] + sums[32 * k + 16 : 32 * k + 24, :]
            imag = sums[32 * k + 8 : 32 * k + 16, :] + sums[32 * k + 24 : 32 * k + 32, :]
            numer = jnp.where(half, real, imag)
            curv = sums[32 * ktiles + 8 * k : 32 * ktiles + 8 * k + 8, :]
            value = gains[at, :]
            pull = rate[at, :]
            gains[at, :] = value + (numer - pull * (value - target[at, :])) / (curv + damp + pull)

    def one_step(step, carry):
        spread_table()
        gather(0, 4)
        vector(0)
        vector(1)
        vector(2)
        vector(3)
        scatter(0, 4)
        update(damping[step])
        return carry

    spread_table()
    for slot in range(group):
        if slot:
            aux_copy(slot, 0).wait_recv()
        hots(slot)
        gather(slot)
        if slot:
            coh_copy(slot, 0).wait_recv()
        vector(slot)
        scatter(slot)
        if slot == 0:
            hear(0, round_z)
            tell(1, round_y)
        elif slot == 1:
            hear(1, round_y)
            tell(2, round_core)
        elif slot == 2:
            hear(2, round_core)
            pl.semaphore_signal(rounds.at[3], inc=1, device_id={"bl": mate}, device_id_type=MESH)
    pl.semaphore_wait(rounds.at[3], 1)
    update(damping[0])
    lax.fori_loop(1, damping.shape[0], one_step, 0)

    pad[0 : 8 * ktiles, :] = gains[...]
    pad[8 * ktiles : 2 * HALF, :] = jnp.zeros((2 * HALF - 8 * ktiles, 2 * HALF), jnp.float32)
    solved = pad[...].T
    gains_all[lane] = solved
    blend = solved + dual[...]
    for owner in range(freqs):
        for part in range(2):
            base = part * HALF + owner * per_owner
            fwd_src[part, owner] = blend[base : base + per_owner, :]

    def far_first(send):
        here = me // plane
        order = sorted(range(planes), key=lambda d: -min(d, planes - d))
        for ahead in order:
            base = lax.rem(here + ahead, planes) * plane

            def one(step, carry):
                send(base + lax.rem(me + step, plane))
                return carry

            lax.fori_loop(0 if ahead else 1, plane, one, 0)

    def fwd_copy(part, other, column, way):
        return pltpu.make_async_remote_copy(
            src_ref=fwd_src.at[part, other],
            dst_ref=fwd_all.at[2 * me + chan],
            send_sem=misc.at[way],
            recv_sem=misc.at[2],
            device_id={"freq": other, "bl": column},
            device_id_type=MESH,
        )

    def send_fwd(other):
        fwd_copy(1 - chan, other, mate, 0).start()
        fwd_copy(chan, other, lane, 1).start()

    far_first(send_fwd)
    fwd_copy(1 - chan, me, mate, 0).start()
    fwd_all[2 * me + chan] = fwd_src[chan, me]

    def gain_copy(slot, off):
        return pltpu.make_async_remote_copy(
            src_ref=gains_all.at[lane],
            dst_ref=gains_all.at[lane],
            send_sem=gain_send.at[slot],
            recv_sem=gain_recv.at[slot],
            device_id={"bl": lax.rem(lane + off, group)},
            device_id_type=MESH,
        )

    for slot in range(1, group):
        gain_copy(slot, OFFSETS[slot]).start()

    def wait_bytes(ref, count, sem):
        view = ref.at[0:count]
        pltpu.make_async_copy(view, view, sem).wait()

    total = 2 * freqs
    basis = bernstein((np.arange(total) + 0.5) / total)
    factor = np.linalg.cholesky(basis.T @ basis)

    def back_copy(other):
        return pltpu.make_async_remote_copy(
            src_ref=back_src.at[other],
            dst_ref=cons_all.at[lane, me],
            send_sem=misc.at[4],
            recv_sem=back_recv.at[me // plane],
            device_id={"freq": other},
            device_id_type=MESH,
        )

    def cons_copy(slot, off, base):
        view = cons_all.at[lane, pl.ds(base, plane)]
        return pltpu.make_async_remote_copy(
            src_ref=view,
            dst_ref=view,
            send_sem=cons_send.at[slot],
            recv_sem=cons_recv.at[slot],
            device_id={"bl": lax.rem(lane + off, group)},
            device_id_type=MESH,
        )

    wait_bytes(fwd_all, total - 1, misc.at[2])
    whole = [None] * 4
    for f in range(total):
        value = fwd_all[f]
        for m in range(4):
            term = value * float(basis[f, m])
            whole[m] = term if whole[m] is None else whole[m] + term
    forward = []
    for row in range(4):
        acc = whole[row]
        for col in range(row):
            acc = acc - float(factor[row, col]) * forward[col]
        forward.append(acc * float(1.0 / factor[row, row]))
    coeffs = [None] * 4
    for row in range(3, -1, -1):
        acc = forward[row]
        for col in range(row + 1, 4):
            acc = acc - float(factor[col, row]) * coeffs[col]
        coeffs[row] = acc * float(1.0 / factor[row, row])
    for f in range(freqs):
        for odd in range(2):
            value = coeffs[0] * float(basis[2 * f + odd, 0])
            for m in range(1, 4):
                value = value + coeffs[m] * float(basis[2 * f + odd, m])
            back_src[f, odd] = value
    far_first(lambda other: back_copy(other).start())
    cons_all[lane, me] = back_src[me]

    def tiles(take):
        for part in range(2):
            for odd in range(2):
                for n in range(stations):
                    take(part, odd, n, n // per_owner, n % per_owner)

    for slot in range(1, group):
        gain_copy(slot, OFFSETS[slot]).wait_recv()

    def emit_gains(part, odd, n, owner, row):
        at = part * HALF + n
        tile = jnp.concatenate([gains_all[odd, at : at + 1, 0:dirs], gains_all[2 + odd, at : at + 1, 0:dirs]], axis=0)
        gains_out[part, odd, n] = -tile

    tiles(emit_gains)

    here = me // plane
    for ahead in sorted(range(planes), key=lambda d: min(d, planes - d)):
        from_plane = lax.rem(here + ahead, planes)
        count = plane if ahead else plane - 1
        view = cons_all.at[lane, pl.ds(from_plane * plane, count)]
        pltpu.make_async_copy(view, view, back_recv.at[from_plane]).wait()
        for slot in range(1, group):
            cons_copy(slot, OFFSETS[slot], from_plane * plane).start()
    for slot in range(1, group):
        wait_bytes(cons_all.at[lax.rem(lane + group - OFFSETS[slot], group)], freqs, cons_recv.at[slot])

    def emit_cons(part, odd, n, owner, row):
        tile = jnp.concatenate(
            [cons_all[part, owner, odd, row : row + 1, 0:dirs], cons_all[2 + part, owner, odd, row : row + 1, 0:dirs]], axis=0
        )
        cons_out[part, odd, n] = -tile

    tiles(emit_cons)

    for slot in range(1, group):
        coh_copy(slot, OFFSETS[slot]).wait_send()
        aux_copy(slot, OFFSETS[slot]).wait_send()
        gain_copy(slot, OFFSETS[slot]).wait_send()
    wait_bytes(fwd_src.at[0], freqs, misc.at[0])
    wait_bytes(fwd_src.at[0], freqs - 1, misc.at[1])
    wait_bytes(back_src, freqs - 1, misc.at[4])
    for slot in range(1, group):
        wait_bytes(cons_all.at[lane], freqs, cons_send.at[slot])


def solution(mesh):
    freqs = mesh.shape["freq"]

    def step(vis, coh, pairs, flags, gains_in, cons_in, dual_in, penalty, damping):
        dirs = gains_in.shape[-2]
        rows = coh.shape[-1]
        ktiles = -(-dirs // 8)
        krows = 8 * ktiles
        term_rows = 32 * ktiles + 16 * (-(-ktiles // 2))
        group = len(OFFSETS)
        per_owner = HALF // freqs
        planes = freqs // min(8, freqs)
        lanes = 2 * HALF
        f32, b16 = jnp.float32, jnp.bfloat16
        whole = pl.BlockSpec(memory_space=pltpu.VMEM)
        scratch = [
            pltpu.VMEM((group - 1, 2 * dirs, rows), f32),
            pltpu.VMEM((group, 2 * dirs, rows), f32),
            pltpu.VMEM((group - 1, 4, rows), f32),
            pltpu.VMEM((group, 4, rows), f32),
            pltpu.VMEM((lanes, 2 * group * rows), b16),
            pltpu.VMEM((2 * group * rows, lanes), b16),
            pltpu.VMEM((2 * krows, 2 * group * rows), f32),
            pltpu.VMEM((term_rows, 2 * group * rows), b16),
            pltpu.VMEM((term_rows, lanes), f32),
            pltpu.VMEM((krows, lanes), f32),
            pltpu.VMEM((krows, lanes), f32),
            pltpu.VMEM((lanes, lanes), f32),
            pltpu.VMEM((krows, lanes), f32),
            pltpu.VMEM((2 * krows, lanes), b16),
            pltpu.VMEM((lanes, lanes), f32),
            pltpu.VMEM((group, lanes, lanes), f32),
            pltpu.VMEM((2, freqs, per_owner, lanes), f32),
            pltpu.VMEM((2 * freqs, per_owner, lanes), f32),
            pltpu.VMEM((freqs, 2, per_owner, lanes), f32),
            pltpu.VMEM((group, freqs, 2, per_owner, lanes), f32),
        ] + [pltpu.SemaphoreType.DMA((n,)) for n in (group,) * 8 + (planes, 8)]
        scratch.append(pltpu.SemaphoreType.REGULAR((4,)))

        def turn(value):
            return jnp.transpose(value, (0, 1, 4, 2, 3))

        dual_whole = dual_in
        gains_in, cons_in, dual_in = turn(gains_in), turn(cons_in), turn(dual_in)
        out = jax.ShapeDtypeStruct(gains_in.shape, f32)
        outs = pl.pallas_call(
            functools.partial(kernel, freqs),
            out_shape=(out, out),
            in_specs=[whole] * 8 + [pl.BlockSpec(memory_space=pltpu.SMEM)],
            out_specs=(whole, whole),
            scratch_shapes=scratch,
            compiler_params=pltpu.CompilerParams(
                collective_id=0, has_side_effects=True, vmem_limit_bytes=40 * 1024 * 1024
            ),
        )(vis, coh, pairs, flags, gains_in, cons_in, dual_in, penalty.reshape(1, dirs), damping)
        minus_gains, minus_cons = (jnp.transpose(value, (0, 1, 3, 4, 2)) for value in outs)
        return (-minus_gains, -minus_cons, dual_whole - minus_gains + minus_cons)

    spread = P(None, "freq", None, None, None)
    return jax.shard_map(
        step,
        mesh=mesh,
        in_specs=(
            P(None, "freq", None, "bl"),
            P(None, "freq", None, None, "bl"),
            P(None, "bl"),
            P("freq", "bl"),
            spread,
            spread,
            spread,
            P(),
            P(),
        ),
        out_specs=(spread, spread, spread),
        check_vma=False,
    )
```

```python
import functools

import jax
import jax.numpy as jnp
import numpy as np
from jax import lax
from jax.experimental import pallas as pl
from jax.experimental.pallas import tpu as pltpu
from jax.sharding import PartitionSpec as P

MESH = pl.DeviceIdType.MESH
OFFSETS = (0, 1, 3, 2)
HALF = 64
WIDE = 256


def bernstein(position):
    other = 1.0 - position
    return np.stack(
        [
            other * other * other,
            3.0 * position * other * other,
            3.0 * position * position * other,
            position * position * position,
        ],
        axis=-1,
    )


def kernel(
    freqs,
    vis,
    coh,
    pairs,
    flags,
    gains_in,
    cons_in,
    dual_in,
    penalty,
    damping,
    gains_out,
    cons_out,
    send_coh,
    coh_all,
    send_aux,
    aux_all,
    hot,
    hot_t,
    picked,
    terms,
    sums,
    gains,
    target,
    dual,
    rate,
    table,
    pad,
    gains_all,
    fwd_src,
    fwd_all,
    back_src,
    cons_all,
    coh_send,
    coh_recv,
    aux_send,
    aux_recv,
    gain_send,
    gain_recv,
    cons_send,
    cons_recv,
    back_recv,
    misc,
    rounds,
):
    stations, dirs = gains_in.shape[2], gains_in.shape[4]
    rows = coh.shape[-1]
    ktiles = gains.shape[0] // 8
    per_owner = HALF // freqs
    plane = min(8, freqs)
    planes = freqs // plane
    even = dirs // 8 * 8
    rest = dirs - even
    me = lax.axis_index("freq")
    lane = lax.axis_index("bl")
    group = len(OFFSETS)

    def place(problem):
        return lax.rem(problem, 2), problem // 2

    deep = max(1, freqs // 8)
    wide = freqs // (2 * deep)

    def freq_at(dz, dy, dc):
        z = lax.rem(me // (2 * wide) + dz, deep)
        y = lax.rem(me // 2 % wide + dy, wide)
        return (z * wide + y) * 2 + lax.rem(me % 2 + dc, 2)

    near = sorted({d % deep for d in (1, 2, -1, -2)} - {0})
    round_z = [freq_at(d, 0, 0) for d in sorted({2 % deep, -2 % deep} - {0})]
    round_y = [freq_at(0, d, 0) for d in range(1, wide)]
    round_core = [freq_at(0, 0, 1)]
    greeted = [freq_at(d, 0, 0) for d in near] + round_y + round_core
    barrier = pltpu.get_barrier_semaphore()
    for off in OFFSETS[1:]:
        other = lax.rem(lane + off, group)
        pl.semaphore_signal(barrier, inc=1, device_id={"bl": other}, device_id_type=MESH)
    for other in greeted:
        pl.semaphore_signal(barrier, inc=1, device_id={"freq": other}, device_id_type=MESH)

    def tell(stage, others):
        for other in others:
            pl.semaphore_signal(rounds.at[stage], inc=1, device_id={"freq": other}, device_id_type=MESH)

    def hear(stage, others):
        if others:
            pl.semaphore_wait(rounds.at[stage], len(others))

    def fill(off, coh_to, aux_to):
        chan, pol = place(lax.rem(lane + off, group))
        weight = flags[pl.ds(chan, 1), :].astype(jnp.float32)
        for part in range(2):
            value = coh[part, chan, pol].astype(jnp.float32) * weight
            coh_to[part * even : (part + 1) * even, :] = value[0:even]
            coh_to[2 * even + part * rest : 2 * even + (part + 1) * rest, :] = value[even:dirs]
            aux_to[part : part + 1, :] = vis[part, chan, pl.ds(pol, 1), :] * weight
            aux_to[2 + part : 3 + part, :] = pairs[part : part + 1, :].astype(jnp.float32)

    def coh_copy(slot, off, at):
        size = WIDE if slot == group - 1 else rows
        sem = slot + at // size
        return pltpu.make_async_remote_copy(
            src_ref=send_coh.at[slot - 1, :, at : at + size],
            dst_ref=coh_all.at[slot, :, at : at + size],
            send_sem=coh_send.at[sem],
            recv_sem=coh_recv.at[sem],
            device_id={"bl": lax.rem(lane + off, group)},
            device_id_type=MESH,
        )

    def aux_copy(slot, off):
        return pltpu.make_async_remote_copy(
            src_ref=send_aux.at[slot - 1],
            dst_ref=aux_all.at[slot],
            send_sem=aux_send.at[slot],
            recv_sem=aux_recv.at[slot],
            device_id={"bl": lax.rem(lane + off, group)},
            device_id_type=MESH,
        )

    for slot in range(1, group):
        fill(OFFSETS[slot], send_coh.at[slot - 1], send_aux.at[slot - 1])
    pl.semaphore_wait(barrier, group - 1 + len(greeted))
    for slot in range(1, group):
        aux_copy(slot, OFFSETS[slot]).start()
    pieces = [(slot, 0) for slot in range(1, group - 1)] + [(group - 1, at) for at in range(0, rows, WIDE)]
    for slot, at in pieces:
        coh_copy(slot, OFFSETS[slot], at).start()
    tell(0, round_z)
    fill(0, coh_all.at[0], aux_all.at[0])

    lanes = lax.broadcasted_iota(jnp.int32, (8 * ktiles, 2 * HALF), 1)
    low = lanes < HALF
    chan, pol = place(lane)
    mate = lane + 1 - 2 * chan

    def pack(ref, to):
        to[...] = jnp.zeros_like(to)
        for part in range(2):
            for n in range(stations):
                to[part * HALF + n : part * HALF + n + 1, 0:dirs] = ref[part, chan, n, pl.ds(pol, 1), :]

    pack(gains_in, pad)
    gains[...] = pad[...].T[0 : 8 * ktiles, :]
    pack(dual_in, dual)
    pack(cons_in, pad)
    target[...] = (pad[...] - dual[...]).T[0 : 8 * ktiles, :]
    pad[...] = jnp.zeros_like(pad)
    pad[0:1, 0:dirs] = penalty[...]
    rate[...] = jnp.broadcast_to(pad[0:1, :], (2 * HALF, 2 * HALF)).T[0 : 8 * ktiles, :]

    def hots(slot):
        ids = lax.broadcasted_iota(jnp.int32, (2 * HALF, rows), 0)
        ids = jnp.where(ids >= HALF, ids - HALF, ids).astype(jnp.float32)
        for part in range(2):
            ones = jnp.where(ids == aux_all[slot, 2 + part : 3 + part, :], 1.0, 0.0)
            at = slice((2 * slot + part) * rows, (2 * slot + part + 1) * rows)
            hot[:, at] = ones.astype(jnp.bfloat16)
            hot_t[at, :] = ones.T.astype(jnp.bfloat16)

    def spread_table():
        value = gains[...]
        high = value.astype(jnp.bfloat16).astype(jnp.float32)
        rest = value - high
        real = jnp.where(low, high, pltpu.roll(rest, HALF, 1))
        imag = jnp.where(low, pltpu.roll(high, HALF, 1), rest)
        for k in range(ktiles):
            both = jnp.concatenate([real[8 * k : 8 * k + 8], imag[8 * k : 8 * k + 8]], axis=0)
            table[16 * k : 16 * k + 16, :] = both.astype(jnp.bfloat16)

    def gather(slot, count=1):
        at = slice(2 * slot * rows, 2 * (slot + count) * rows)
        picked[:, at] = jnp.dot(table[...], hot[:, at], preferred_element_type=jnp.float32)

    def vector(slot, start=0, stop=rows):
        for at in range(start, stop, WIDE):
            sample = slice(at, at + WIDE)
            first = slice(2 * slot * rows + at, 2 * slot * rows + at + WIDE)
            second = slice((2 * slot + 1) * rows + at, (2 * slot + 1) * rows + at + WIDE)

            def load(k):
                if 8 * k < even:
                    cre = coh_all[slot, 8 * k : 8 * k + 8, sample]
                    cim = coh_all[slot, even + 8 * k : even + 8 * k + 8, sample]
                else:
                    cre = coh_all[slot, 2 * even : 2 * even + 8, sample]
                    cim = pltpu.roll(cre, rest, 0)
                pre = picked[16 * k : 16 * k + 8, first]
                pim = picked[16 * k + 8 : 16 * k + 16, first]
                qre = picked[16 * k : 16 * k + 8, second]
                qim = picked[16 * k + 8 : 16 * k + 16, second]
                return cre, cim, pre, pim, qre, qim

            mre = jnp.zeros((8, WIDE), jnp.float32)
            mim = jnp.zeros((8, WIDE), jnp.float32)
            for k in range(ktiles):
                cre, cim, pre, pim, qre, qim = load(k)
                tre = cre * qre + cim * qim
                tim = cim * qre - cre * qim
                mre = mre + (pre * tre - pim * tim)
                mim = mim + (pre * tim + pim * tre)
            rre = aux_all[slot, 0:1, sample] - jnp.sum(mre, axis=0, keepdims=True)
            rim = aux_all[slot, 1:2, sample] - jnp.sum(mim, axis=0, keepdims=True)
            rre = jnp.broadcast_to(rre, (8, WIDE))
            rim = jnp.broadcast_to(rim, (8, WIDE))
            for k in range(ktiles):
                cre, cim, pre, pim, qre, qim = load(k)
                are = rre * cre + rim * cim
                aim = rim * cre - rre * cim
                square = cre * cre + cim * cim
                sides = (
                    (first, are * qre - aim * qim, are * qim + aim * qre, square * (qre * qre + qim * qim)),
                    (second, are * pre + aim * pim, are * pim - aim * pre, square * (pre * pre + pim * pim)),
                )
                for cols, real, imag, curv in sides:
                    both = jnp.concatenate([real, imag], axis=0)
                    high = both.astype(jnp.bfloat16)
                    terms[48 * k : 48 * k + 16, cols] = high
                    terms[48 * k + 16 : 48 * k + 32, cols] = (both - high.astype(jnp.float32)).astype(jnp.bfloat16)
                    left = curv - curv.astype(jnp.bfloat16).astype(jnp.float32)
                    both = jnp.concatenate([curv, left], axis=0)
                    terms[48 * k + 32 : 48 * k + 48, cols] = both.astype(jnp.bfloat16)

    def scatter(slot, count=1):
        at = slice(2 * slot * rows, 2 * (slot + count) * rows)
        value = jnp.dot(terms[:, at], hot_t[at, :], preferred_element_type=jnp.float32)
        sums[...] = value if slot == 0 else sums[...] + value

    def update(damp):
        half = lax.broadcasted_iota(jnp.int32, (8, 2 * HALF), 1) < HALF
        for k in range(ktiles):
            at = slice(8 * k, 8 * k + 8)
            real = sums[48 * k : 48 * k + 8, :] + sums[48 * k + 16 : 48 * k + 24, :]
            imag = sums[48 * k + 8 : 48 * k + 16, :] + sums[48 * k + 24 : 48 * k + 32, :]
            numer = jnp.where(half, real, imag)
            curv = sums[48 * k + 32 : 48 * k + 40, :] + sums[48 * k + 40 : 48 * k + 48, :]
            value = gains[at, :]
            pull = rate[at, :]
            gains[at, :] = value + (numer - pull * (value - target[at, :])) / (curv + damp + pull)

    def one_step(step, carry):
        spread_table()
        gather(0, 4)
        vector(0)
        vector(1)
        vector(2)
        vector(3)
        scatter(0, 4)
        update(damping[step])
        return carry

    spread_table()
    for slot in range(group):
        if slot:
            aux_copy(slot, 0).wait_recv()
        hots(slot)
        gather(slot)
        if slot == group - 1:
            for at in range(0, rows, WIDE):
                coh_copy(slot, 0, at).wait_recv()
                vector(slot, at, at + WIDE)
                for part in range(2):
                    base = (2 * slot + part) * rows + at
                    cols = slice(base, base + WIDE)
                    sums[...] += jnp.dot(terms[:, cols], hot_t[cols, :], preferred_element_type=jnp.float32)
            continue
        if slot:
            coh_copy(slot, 0, 0).wait_recv()
        vector(slot)
        scatter(slot)
        if slot == 0:
            hear(0, round_z)
            tell(1, round_y)
        elif slot == 1:
            hear(1, round_y)
            tell(2, round_core)
        elif slot == 2:
            hear(2, round_core)
            pl.semaphore_signal(rounds.at[3], inc=1, device_id={"bl": mate}, device_id_type=MESH)
    pl.semaphore_wait(rounds.at[3], 1)
    update(damping[0])
    lax.fori_loop(1, damping.shape[0], one_step, 0)

    pad[0 : 8 * ktiles, :] = gains[...]
    pad[8 * ktiles : 2 * HALF, :] = jnp.zeros((2 * HALF - 8 * ktiles, 2 * HALF), jnp.float32)
    solved = pad[...].T
    gains_all[lane] = solved
    blend = solved + dual[...]
    for owner in range(freqs):
        for part in range(2):
            base = part * HALF + owner * per_owner
            fwd_src[part, owner] = blend[base : base + per_owner, :]

    def far_first(send):
        here = me // plane
        order = sorted(range(planes), key=lambda d: -min(d, planes - d))
        for ahead in order:
            base = lax.rem(here + ahead, planes) * plane

            def one(step, carry):
                send(base + lax.rem(me + step, plane))
                return carry

            lax.fori_loop(0 if ahead else 1, plane, one, 0)

    def fwd_copy(part, other, column, way):
        return pltpu.make_async_remote_copy(
            src_ref=fwd_src.at[part, other],
            dst_ref=fwd_all.at[2 * me + chan],
            send_sem=misc.at[way],
            recv_sem=misc.at[2],
            device_id={"freq": other, "bl": column},
            device_id_type=MESH,
        )

    def send_fwd(other):
        fwd_copy(1 - chan, other, mate, 0).start()
        fwd_copy(chan, other, lane, 1).start()

    far_first(send_fwd)
    fwd_copy(1 - chan, me, mate, 0).start()
    fwd_all[2 * me + chan] = fwd_src[chan, me]

    def gain_copy(slot, off):
        return pltpu.make_async_remote_copy(
            src_ref=gains_all.at[lane],
            dst_ref=gains_all.at[lane],
            send_sem=gain_send.at[slot],
            recv_sem=gain_recv.at[slot],
            device_id={"bl": lax.rem(lane + off, group)},
            device_id_type=MESH,
        )

    def wait_bytes(ref, count, sem):
        view = ref.at[0:count]
        pltpu.make_async_copy(view, view, sem).wait()

    total = 2 * freqs
    basis = bernstein((np.arange(total) + 0.5) / total)
    factor = np.linalg.cholesky(basis.T @ basis)

    def back_copy(other):
        return pltpu.make_async_remote_copy(
            src_ref=back_src.at[other],
            dst_ref=cons_all.at[lane, me],
            send_sem=misc.at[4],
            recv_sem=back_recv.at[me // plane],
            device_id={"freq": other},
            device_id_type=MESH,
        )

    def cons_copy(slot, off, base):
        view = cons_all.at[lane, pl.ds(base, plane)]
        return pltpu.make_async_remote_copy(
            src_ref=view,
            dst_ref=view,
            send_sem=cons_send.at[slot],
            recv_sem=cons_recv.at[slot],
            device_id={"bl": lax.rem(lane + off, group)},
            device_id_type=MESH,
        )

    wait_bytes(fwd_all, total - 1, misc.at[2])
    chains = [[None] * 4 for _ in range(4)]
    for f in range(total):
        value = fwd_all[f]
        for m in range(4):
            term = value * float(basis[f, m])
            held = chains[m][f % 4]
            chains[m][f % 4] = term if held is None else held + term
    whole = [(c[0] + c[1]) + (c[2] + c[3]) for c in chains]
    forward = []
    for row in range(4):
        acc = whole[row]
        for col in range(row):
            acc = acc - float(factor[row, col]) * forward[col]
        forward.append(acc * float(1.0 / factor[row, row]))
    coeffs = [None] * 4
    for row in range(3, -1, -1):
        acc = forward[row]
        for col in range(row + 1, 4):
            acc = acc - float(factor[col, row]) * coeffs[col]
        coeffs[row] = acc * float(1.0 / factor[row, row])
    for f in range(freqs):
        for odd in range(2):
            value = coeffs[0] * float(basis[2 * f + odd, 0])
            for m in range(1, 4):
                value = value + coeffs[m] * float(basis[2 * f + odd, m])
            back_src[f, odd] = value
    far_first(lambda other: back_copy(other).start())
    for slot in range(1, group):
        gain_copy(slot, OFFSETS[slot]).start()
    cons_all[lane, me] = back_src[me]

    def tiles(take):
        for part in range(2):
            for odd in range(2):
                for n in range(stations):
                    take(part, odd, n, n // per_owner, n % per_owner)

    def emit_gains(part, odd, n, owner, row):
        at = part * HALF + n
        tile = jnp.concatenate([gains_all[odd, at : at + 1, 0:dirs], gains_all[2 + odd, at : at + 1, 0:dirs]], axis=0)
        gains_out[part, odd, n] = -tile

    here = me // plane
    for ahead in sorted(range(planes), key=lambda d: min(d, planes - d)):
        from_plane = lax.rem(here + ahead, planes)
        count = plane if ahead else plane - 1
        view = cons_all.at[lane, pl.ds(from_plane * plane, count)]
        pltpu.make_async_copy(view, view, back_recv.at[from_plane]).wait()
        for slot in range(1, group):
            cons_copy(slot, OFFSETS[slot], from_plane * plane).start()
    for slot in range(1, group):
        gain_copy(slot, OFFSETS[slot]).wait_recv()
    tiles(emit_gains)
    for slot in range(1, group):
        wait_bytes(cons_all.at[lax.rem(lane + group - OFFSETS[slot], group)], freqs, cons_recv.at[slot])

    def emit_cons(part, odd, n, owner, row):
        tile = jnp.concatenate(
            [cons_all[part, owner, odd, row : row + 1, 0:dirs], cons_all[2 + part, owner, odd, row : row + 1, 0:dirs]], axis=0
        )
        cons_out[part, odd, n] = -tile

    tiles(emit_cons)

    for slot, at in pieces:
        coh_copy(slot, OFFSETS[slot], at).wait_send()
    for slot in range(1, group):
        aux_copy(slot, OFFSETS[slot]).wait_send()
        gain_copy(slot, OFFSETS[slot]).wait_send()
    wait_bytes(fwd_src.at[0], freqs, misc.at[0])
    wait_bytes(fwd_src.at[0], freqs - 1, misc.at[1])
    wait_bytes(back_src, freqs - 1, misc.at[4])
    for slot in range(1, group):
        wait_bytes(cons_all.at[lane], freqs, cons_send.at[slot])


def solution(mesh):
    freqs = mesh.shape["freq"]

    def step(vis, coh, pairs, flags, gains_in, cons_in, dual_in, penalty, damping):
        dirs = gains_in.shape[-2]
        rows = coh.shape[-1]
        ktiles = -(-dirs // 8)
        krows = 8 * ktiles
        term_rows = 48 * ktiles
        group = len(OFFSETS)
        per_owner = HALF // freqs
        planes = freqs // min(8, freqs)
        lanes = 2 * HALF
        f32, b16 = jnp.float32, jnp.bfloat16
        whole = pl.BlockSpec(memory_space=pltpu.VMEM)
        scratch = [
            pltpu.VMEM((group - 1, 2 * dirs, rows), f32),
            pltpu.VMEM((group, 2 * dirs, rows), f32),
            pltpu.VMEM((group - 1, 4, rows), f32),
            pltpu.VMEM((group, 4, rows), f32),
            pltpu.VMEM((lanes, 2 * group * rows), b16),
            pltpu.VMEM((2 * group * rows, lanes), b16),
            pltpu.VMEM((2 * krows, 2 * group * rows), f32),
            pltpu.VMEM((term_rows, 2 * group * rows), b16),
            pltpu.VMEM((term_rows, lanes), f32),
            pltpu.VMEM((krows, lanes), f32),
            pltpu.VMEM((krows, lanes), f32),
            pltpu.VMEM((lanes, lanes), f32),
            pltpu.VMEM((krows, lanes), f32),
            pltpu.VMEM((2 * krows, lanes), b16),
            pltpu.VMEM((lanes, lanes), f32),
            pltpu.VMEM((group, lanes, lanes), f32),
            pltpu.VMEM((2, freqs, per_owner, lanes), f32),
            pltpu.VMEM((2 * freqs, per_owner, lanes), f32),
            pltpu.VMEM((freqs, 2, per_owner, lanes), f32),
            pltpu.VMEM((group, freqs, 2, per_owner, lanes), f32),
        ] + [pltpu.SemaphoreType.DMA((n,)) for n in (group - 1 + rows // WIDE,) * 2 + (group,) * 6 + (planes, 8)]
        scratch.append(pltpu.SemaphoreType.REGULAR((4,)))

        def turn(value):
            return jnp.transpose(value, (0, 1, 4, 2, 3))

        dual_whole = dual_in
        gains_in, cons_in, dual_in = turn(gains_in), turn(cons_in), turn(dual_in)
        out = jax.ShapeDtypeStruct(gains_in.shape, f32)
        outs = pl.pallas_call(
            functools.partial(kernel, freqs),
            out_shape=(out, out),
            in_specs=[whole] * 8 + [pl.BlockSpec(memory_space=pltpu.SMEM)],
            out_specs=(whole, whole),
            scratch_shapes=scratch,
            compiler_params=pltpu.CompilerParams(
                collective_id=0, has_side_effects=True, vmem_limit_bytes=40 * 1024 * 1024
            ),
        )(vis, coh, pairs, flags, gains_in, cons_in, dual_in, penalty.reshape(1, dirs), damping)
        minus_gains, minus_cons = (jnp.transpose(value, (0, 1, 3, 4, 2)) for value in outs)
        return (-minus_gains, -minus_cons, dual_whole - minus_gains + minus_cons)

    spread = P(None, "freq", None, None, None)
    return jax.shard_map(
        step,
        mesh=mesh,
        in_specs=(
            P(None, "freq", None, "bl"),
            P(None, "freq", None, None, "bl"),
            P(None, "bl"),
            P("freq", "bl"),
            spread,
            spread,
            spread,
            P(),
            P(),
        ),
        out_specs=(spread, spread, spread),
        check_vma=False,
    )
```

```python
import functools

import jax
import jax.numpy as jnp
import numpy as np
from jax import lax
from jax.experimental import pallas as pl
from jax.experimental.pallas import tpu as pltpu
from jax.sharding import PartitionSpec as P

MESH = pl.DeviceIdType.MESH
OFFSETS = (0, 1, 3, 2)
HALF = 64
WIDE = 256


def bernstein(position):
    other = 1.0 - position
    return np.stack(
        [
            other * other * other,
            3.0 * position * other * other,
            3.0 * position * position * other,
            position * position * position,
        ],
        axis=-1,
    )


def kernel(
    freqs,
    vis,
    coh,
    pairs,
    flags,
    gains_in,
    cons_in,
    dual_in,
    penalty,
    damping,
    gains_out,
    cons_out,
    send_coh,
    coh_all,
    send_aux,
    aux_all,
    hot,
    hot_t,
    picked,
    terms,
    sums,
    gains,
    target,
    dual,
    rate,
    table,
    pad,
    gains_all,
    fwd_src,
    fwd_all,
    back_src,
    cons_all,
    coh_send,
    coh_recv,
    aux_send,
    aux_recv,
    gain_send,
    gain_recv,
    cons_send,
    cons_recv,
    back_recv,
    misc,
    rounds,
):
    stations, dirs = gains_in.shape[2], gains_in.shape[4]
    rows = coh.shape[-1]
    ktiles = gains.shape[0] // 8
    per_owner = HALF // freqs
    plane = min(8, freqs)
    planes = freqs // plane
    even = dirs // 8 * 8
    rest = dirs - even
    me = lax.axis_index("freq")
    lane = lax.axis_index("bl")
    group = len(OFFSETS)

    def place(problem):
        return lax.rem(problem, 2), problem // 2

    deep = max(1, freqs // 8)
    wide = freqs // (2 * deep)

    def freq_at(dz, dy, dc):
        z = lax.rem(me // (2 * wide) + dz, deep)
        y = lax.rem(me // 2 % wide + dy, wide)
        return (z * wide + y) * 2 + lax.rem(me % 2 + dc, 2)

    near = sorted({d % deep for d in (1, 2, -1, -2)} - {0})
    round_z = [freq_at(d, 0, 0) for d in sorted({2 % deep, -2 % deep} - {0})]
    round_y = [freq_at(0, d, 0) for d in range(1, wide)]
    round_core = [freq_at(0, 0, 1)]
    greeted = [freq_at(d, 0, 0) for d in near] + round_y + round_core
    barrier = pltpu.get_barrier_semaphore()
    for off in OFFSETS[1:]:
        other = lax.rem(lane + off, group)
        pl.semaphore_signal(barrier, inc=1, device_id={"bl": other}, device_id_type=MESH)
    for other in greeted:
        pl.semaphore_signal(barrier, inc=1, device_id={"freq": other}, device_id_type=MESH)

    def tell(stage, others):
        for other in others:
            pl.semaphore_signal(rounds.at[stage], inc=1, device_id={"freq": other}, device_id_type=MESH)

    def hear(stage, others):
        if others:
            pl.semaphore_wait(rounds.at[stage], len(others))

    def fill(off, coh_to, aux_to):
        chan, pol = place(lax.rem(lane + off, group))
        weight = flags[pl.ds(chan, 1), :].astype(jnp.float32)
        for part in range(2):
            value = coh[part, chan, pol].astype(jnp.float32) * weight
            coh_to[part * even : (part + 1) * even, :] = value[0:even]
            coh_to[2 * even + part * rest : 2 * even + (part + 1) * rest, :] = value[even:dirs]
            aux_to[part : part + 1, :] = vis[part, chan, pl.ds(pol, 1), :] * weight
            aux_to[2 + part : 3 + part, :] = pairs[part : part + 1, :].astype(jnp.float32)

    def coh_copy(slot, off, at):
        size = WIDE if slot == group - 1 else rows
        sem = slot + at // size
        return pltpu.make_async_remote_copy(
            src_ref=send_coh.at[slot - 1, :, at : at + size],
            dst_ref=coh_all.at[slot, :, at : at + size],
            send_sem=coh_send.at[sem],
            recv_sem=coh_recv.at[sem],
            device_id={"bl": lax.rem(lane + off, group)},
            device_id_type=MESH,
        )

    def aux_copy(slot, off):
        return pltpu.make_async_remote_copy(
            src_ref=send_aux.at[slot - 1],
            dst_ref=aux_all.at[slot],
            send_sem=aux_send.at[slot],
            recv_sem=aux_recv.at[slot],
            device_id={"bl": lax.rem(lane + off, group)},
            device_id_type=MESH,
        )

    for slot in range(1, group):
        fill(OFFSETS[slot], send_coh.at[slot - 1], send_aux.at[slot - 1])
    pl.semaphore_wait(barrier, group - 1 + len(greeted))
    for slot in range(1, group):
        aux_copy(slot, OFFSETS[slot]).start()
    pieces = [(slot, 0) for slot in range(1, group - 1)] + [(group - 1, at) for at in range(0, rows, WIDE)]
    for slot, at in pieces:
        coh_copy(slot, OFFSETS[slot], at).start()
    tell(0, round_z)
    fill(0, coh_all.at[0], aux_all.at[0])

    lanes = lax.broadcasted_iota(jnp.int32, (8 * ktiles, 2 * HALF), 1)
    low = lanes < HALF
    chan, pol = place(lane)
    mate = lane + 1 - 2 * chan

    def pack(ref, to):
        to[...] = jnp.zeros_like(to)
        for part in range(2):
            for n in range(stations):
                to[part * HALF + n : part * HALF + n + 1, 0:dirs] = ref[part, chan, n, pl.ds(pol, 1), :]

    pack(gains_in, pad)
    gains[...] = pad[...].T[0 : 8 * ktiles, :]
    pack(dual_in, dual)
    pack(cons_in, pad)
    target[...] = (pad[...] - dual[...]).T[0 : 8 * ktiles, :]
    pad[...] = jnp.zeros_like(pad)
    pad[0:1, 0:dirs] = penalty[...]
    rate[...] = jnp.broadcast_to(pad[0:1, :], (2 * HALF, 2 * HALF)).T[0 : 8 * ktiles, :]

    def hots(slot):
        ids = lax.broadcasted_iota(jnp.int32, (2 * HALF, rows), 0)
        ids = jnp.where(ids >= HALF, ids - HALF, ids).astype(jnp.float32)
        for part in range(2):
            ones = jnp.where(ids == aux_all[slot, 2 + part : 3 + part, :], 1.0, 0.0)
            at = slice((2 * slot + part) * rows, (2 * slot + part + 1) * rows)
            hot[:, at] = ones.astype(jnp.bfloat16)
            hot_t[at, :] = ones.T.astype(jnp.bfloat16)

    def spread_table():
        value = gains[...]
        high = value.astype(jnp.bfloat16).astype(jnp.float32)
        rest = value - high
        real = jnp.where(low, high, pltpu.roll(rest, HALF, 1))
        imag = jnp.where(low, pltpu.roll(high, HALF, 1), rest)
        for k in range(ktiles):
            both = jnp.concatenate([real[8 * k : 8 * k + 8], imag[8 * k : 8 * k + 8]], axis=0)
            table[16 * k : 16 * k + 16, :] = both.astype(jnp.bfloat16)

    def gather(slot, count=1):
        at = slice(2 * slot * rows, 2 * (slot + count) * rows)
        picked[:, at] = jnp.dot(table[...], hot[:, at], preferred_element_type=jnp.float32)

    def vector(slot, start=0, stop=rows):
        for at in range(start, stop, WIDE):
            sample = slice(at, at + WIDE)
            first = slice(2 * slot * rows + at, 2 * slot * rows + at + WIDE)
            second = slice((2 * slot + 1) * rows + at, (2 * slot + 1) * rows + at + WIDE)

            def load(k):
                if 8 * k < even:
                    cre = coh_all[slot, 8 * k : 8 * k + 8, sample]
                    cim = coh_all[slot, even + 8 * k : even + 8 * k + 8, sample]
                else:
                    cre = coh_all[slot, 2 * even : 2 * even + 8, sample]
                    cim = pltpu.roll(cre, rest, 0)
                pre = picked[16 * k : 16 * k + 8, first]
                pim = picked[16 * k + 8 : 16 * k + 16, first]
                qre = picked[16 * k : 16 * k + 8, second]
                qim = picked[16 * k + 8 : 16 * k + 16, second]
                return cre, cim, pre, pim, qre, qim

            mre = jnp.zeros((8, WIDE), jnp.float32)
            mim = jnp.zeros((8, WIDE), jnp.float32)
            for k in range(ktiles):
                cre, cim, pre, pim, qre, qim = load(k)
                tre = cre * qre + cim * qim
                tim = cim * qre - cre * qim
                mre = mre + (pre * tre - pim * tim)
                mim = mim + (pre * tim + pim * tre)
            rre = aux_all[slot, 0:1, sample] - jnp.sum(mre, axis=0, keepdims=True)
            rim = aux_all[slot, 1:2, sample] - jnp.sum(mim, axis=0, keepdims=True)
            rre = jnp.broadcast_to(rre, (8, WIDE))
            rim = jnp.broadcast_to(rim, (8, WIDE))
            for k in range(ktiles):
                cre, cim, pre, pim, qre, qim = load(k)
                are = rre * cre + rim * cim
                aim = rim * cre - rre * cim
                square = cre * cre + cim * cim
                sides = (
                    (first, are * qre - aim * qim, are * qim + aim * qre, square * (qre * qre + qim * qim)),
                    (second, are * pre + aim * pim, are * pim - aim * pre, square * (pre * pre + pim * pim)),
                )
                for cols, real, imag, curv in sides:
                    both = jnp.concatenate([real, imag], axis=0)
                    high = both.astype(jnp.bfloat16)
                    terms[48 * k : 48 * k + 16, cols] = high
                    terms[48 * k + 16 : 48 * k + 32, cols] = (both - high.astype(jnp.float32)).astype(jnp.bfloat16)
                    left = curv - curv.astype(jnp.bfloat16).astype(jnp.float32)
                    both = jnp.concatenate([curv, left], axis=0)
                    terms[48 * k + 32 : 48 * k + 48, cols] = both.astype(jnp.bfloat16)

    def scatter(slot, count=1):
        at = slice(2 * slot * rows, 2 * (slot + count) * rows)
        value = jnp.dot(terms[:, at], hot_t[at, :], preferred_element_type=jnp.float32)
        sums[...] = value if slot == 0 else sums[...] + value

    def update(damp):
        half = lax.broadcasted_iota(jnp.int32, (8, 2 * HALF), 1) < HALF
        for k in range(ktiles):
            at = slice(8 * k, 8 * k + 8)
            real = sums[48 * k : 48 * k + 8, :] + sums[48 * k + 16 : 48 * k + 24, :]
            imag = sums[48 * k + 8 : 48 * k + 16, :] + sums[48 * k + 24 : 48 * k + 32, :]
            numer = jnp.where(half, real, imag)
            curv = sums[48 * k + 32 : 48 * k + 40, :] + sums[48 * k + 40 : 48 * k + 48, :]
            value = gains[at, :]
            pull = rate[at, :]
            gains[at, :] = value + (numer - pull * (value - target[at, :])) / (curv + damp + pull)

    def one_step(step, carry):
        spread_table()
        gather(0)
        gather(1, 3)
        vector(0)
        scatter(0)
        vector(1)
        scatter(1)
        vector(2)
        scatter(2)
        vector(3)
        scatter(3)
        update(damping[step])
        return carry

    spread_table()
    for slot in range(group):
        if slot:
            aux_copy(slot, 0).wait_recv()
        hots(slot)
        gather(slot)
        if slot == group - 1:
            for at in range(0, rows, WIDE):
                coh_copy(slot, 0, at).wait_recv()
                vector(slot, at, at + WIDE)
                for part in range(2):
                    base = (2 * slot + part) * rows + at
                    cols = slice(base, base + WIDE)
                    sums[...] += jnp.dot(terms[:, cols], hot_t[cols, :], preferred_element_type=jnp.float32)
            continue
        if slot:
            coh_copy(slot, 0, 0).wait_recv()
        vector(slot)
        scatter(slot)
        if slot == 0:
            hear(0, round_z)
            tell(1, round_y)
        elif slot == 1:
            hear(1, round_y)
            tell(2, round_core)
        elif slot == 2:
            hear(2, round_core)
            pl.semaphore_signal(rounds.at[3], inc=1, device_id={"bl": mate}, device_id_type=MESH)
    pl.semaphore_wait(rounds.at[3], 1)
    update(damping[0])
    lax.fori_loop(1, damping.shape[0], one_step, 0)

    pad[0 : 8 * ktiles, :] = gains[...]
    pad[8 * ktiles : 2 * HALF, :] = jnp.zeros((2 * HALF - 8 * ktiles, 2 * HALF), jnp.float32)
    solved = pad[...].T
    gains_all[lane] = solved
    blend = solved + dual[...]
    for owner in range(freqs):
        for part in range(2):
            base = part * HALF + owner * per_owner
            fwd_src[part, owner] = blend[base : base + per_owner, :]

    def far_first(send):
        here = me // plane
        order = sorted(range(planes), key=lambda d: -min(d, planes - d))
        for ahead in order:
            base = lax.rem(here + ahead, planes) * plane

            def one(step, carry):
                send(base + lax.rem(me + step, plane))
                return carry

            lax.fori_loop(0 if ahead else 1, plane, one, 0)

    def fwd_copy(part, other, column, way):
        return pltpu.make_async_remote_copy(
            src_ref=fwd_src.at[part, other],
            dst_ref=fwd_all.at[2 * me + chan],
            send_sem=misc.at[way],
            recv_sem=misc.at[2],
            device_id={"freq": other, "bl": column},
            device_id_type=MESH,
        )

    def send_fwd(other):
        fwd_copy(1 - chan, other, mate, 0).start()
        fwd_copy(chan, other, lane, 1).start()

    far_first(send_fwd)
    fwd_copy(1 - chan, me, mate, 0).start()
    fwd_all[2 * me + chan] = fwd_src[chan, me]

    def gain_copy(slot, off):
        return pltpu.make_async_remote_copy(
            src_ref=gains_all.at[lane],
            dst_ref=gains_all.at[lane],
            send_sem=gain_send.at[slot],
            recv_sem=gain_recv.at[slot],
            device_id={"bl": lax.rem(lane + off, group)},
            device_id_type=MESH,
        )

    def wait_bytes(ref, count, sem):
        view = ref.at[0:count]
        pltpu.make_async_copy(view, view, sem).wait()

    total = 2 * freqs
    basis = bernstein((np.arange(total) + 0.5) / total)
    factor = np.linalg.cholesky(basis.T @ basis)

    def back_copy(other):
        return pltpu.make_async_remote_copy(
            src_ref=back_src.at[other],
            dst_ref=cons_all.at[lane, me],
            send_sem=misc.at[4],
            recv_sem=back_recv.at[me // plane],
            device_id={"freq": other},
            device_id_type=MESH,
        )

    def cons_copy(slot, off, base):
        view = cons_all.at[lane, pl.ds(base, plane)]
        return pltpu.make_async_remote_copy(
            src_ref=view,
            dst_ref=view,
            send_sem=cons_send.at[slot],
            recv_sem=cons_recv.at[slot],
            device_id={"bl": lax.rem(lane + off, group)},
            device_id_type=MESH,
        )

    wait_bytes(fwd_all, total - 1, misc.at[2])
    chains = [[None] * 4 for _ in range(4)]
    for f in range(total):
        value = fwd_all[f]
        for m in range(4):
            term = value * float(basis[f, m])
            held = chains[m][f % 4]
            chains[m][f % 4] = term if held is None else held + term
    whole = [(c[0] + c[1]) + (c[2] + c[3]) for c in chains]
    forward = []
    for row in range(4):
        acc = whole[row]
        for col in range(row):
            acc = acc - float(factor[row, col]) * forward[col]
        forward.append(acc * float(1.0 / factor[row, row]))
    coeffs = [None] * 4
    for row in range(3, -1, -1):
        acc = forward[row]
        for col in range(row + 1, 4):
            acc = acc - float(factor[col, row]) * coeffs[col]
        coeffs[row] = acc * float(1.0 / factor[row, row])
    for f in range(freqs):
        for odd in range(2):
            value = coeffs[0] * float(basis[2 * f + odd, 0])
            for m in range(1, 4):
                value = value + coeffs[m] * float(basis[2 * f + odd, m])
            back_src[f, odd] = value
    far_first(lambda other: back_copy(other).start())
    for slot in range(1, group):
        gain_copy(slot, OFFSETS[slot]).start()
    cons_all[lane, me] = back_src[me]

    def tiles(take):
        for part in range(2):
            for odd in range(2):
                for n in range(stations):
                    take(part, odd, n, n // per_owner, n % per_owner)

    def emit_gains(part, odd, n, owner, row):
        at = part * HALF + n
        tile = jnp.concatenate([gains_all[odd, at : at + 1, 0:dirs], gains_all[2 + odd, at : at + 1, 0:dirs]], axis=0)
        gains_out[part, odd, n] = -tile

    here = me // plane
    for ahead in sorted(range(planes), key=lambda d: min(d, planes - d)):
        from_plane = lax.rem(here + ahead, planes)
        count = plane if ahead else plane - 1
        view = cons_all.at[lane, pl.ds(from_plane * plane, count)]
        pltpu.make_async_copy(view, view, back_recv.at[from_plane]).wait()
        for slot in range(1, group):
            cons_copy(slot, OFFSETS[slot], from_plane * plane).start()
    for slot in range(1, group):
        gain_copy(slot, OFFSETS[slot]).wait_recv()
    tiles(emit_gains)
    for slot in range(1, group):
        wait_bytes(cons_all.at[lax.rem(lane + group - OFFSETS[slot], group)], freqs, cons_recv.at[slot])

    def emit_cons(part, odd, n, owner, row):
        tile = jnp.concatenate(
            [cons_all[part, owner, odd, row : row + 1, 0:dirs], cons_all[2 + part, owner, odd, row : row + 1, 0:dirs]], axis=0
        )
        cons_out[part, odd, n] = -tile

    tiles(emit_cons)

    for slot, at in pieces:
        coh_copy(slot, OFFSETS[slot], at).wait_send()
    for slot in range(1, group):
        aux_copy(slot, OFFSETS[slot]).wait_send()
        gain_copy(slot, OFFSETS[slot]).wait_send()
    wait_bytes(fwd_src.at[0], freqs, misc.at[0])
    wait_bytes(fwd_src.at[0], freqs - 1, misc.at[1])
    wait_bytes(back_src, freqs - 1, misc.at[4])
    for slot in range(1, group):
        wait_bytes(cons_all.at[lane], freqs, cons_send.at[slot])


def solution(mesh):
    freqs = mesh.shape["freq"]

    def step(vis, coh, pairs, flags, gains_in, cons_in, dual_in, penalty, damping):
        dirs = gains_in.shape[-2]
        rows = coh.shape[-1]
        ktiles = -(-dirs // 8)
        krows = 8 * ktiles
        term_rows = 48 * ktiles
        group = len(OFFSETS)
        per_owner = HALF // freqs
        planes = freqs // min(8, freqs)
        lanes = 2 * HALF
        f32, b16 = jnp.float32, jnp.bfloat16
        whole = pl.BlockSpec(memory_space=pltpu.VMEM)
        scratch = [
            pltpu.VMEM((group - 1, 2 * dirs, rows), f32),
            pltpu.VMEM((group, 2 * dirs, rows), f32),
            pltpu.VMEM((group - 1, 4, rows), f32),
            pltpu.VMEM((group, 4, rows), f32),
            pltpu.VMEM((lanes, 2 * group * rows), b16),
            pltpu.VMEM((2 * group * rows, lanes), b16),
            pltpu.VMEM((2 * krows, 2 * group * rows), f32),
            pltpu.VMEM((term_rows, 2 * group * rows), b16),
            pltpu.VMEM((term_rows, lanes), f32),
            pltpu.VMEM((krows, lanes), f32),
            pltpu.VMEM((krows, lanes), f32),
            pltpu.VMEM((lanes, lanes), f32),
            pltpu.VMEM((krows, lanes), f32),
            pltpu.VMEM((2 * krows, lanes), b16),
            pltpu.VMEM((lanes, lanes), f32),
            pltpu.VMEM((group, lanes, lanes), f32),
            pltpu.VMEM((2, freqs, per_owner, lanes), f32),
            pltpu.VMEM((2 * freqs, per_owner, lanes), f32),
            pltpu.VMEM((freqs, 2, per_owner, lanes), f32),
            pltpu.VMEM((group, freqs, 2, per_owner, lanes), f32),
        ] + [pltpu.SemaphoreType.DMA((n,)) for n in (group - 1 + rows // WIDE,) * 2 + (group,) * 6 + (planes, 8)]
        scratch.append(pltpu.SemaphoreType.REGULAR((4,)))

        def turn(value):
            return jnp.transpose(value, (0, 1, 4, 2, 3))

        dual_whole = dual_in
        gains_in, cons_in, dual_in = turn(gains_in), turn(cons_in), turn(dual_in)
        out = jax.ShapeDtypeStruct(gains_in.shape, f32)
        outs = pl.pallas_call(
            functools.partial(kernel, freqs),
            out_shape=(out, out),
            in_specs=[whole] * 8 + [pl.BlockSpec(memory_space=pltpu.SMEM)],
            out_specs=(whole, whole),
            scratch_shapes=scratch,
            compiler_params=pltpu.CompilerParams(
                collective_id=0, has_side_effects=True, vmem_limit_bytes=40 * 1024 * 1024
            ),
        )(vis, coh, pairs, flags, gains_in, cons_in, dual_in, penalty.reshape(1, dirs), damping)
        minus_gains, minus_cons = (jnp.transpose(value, (0, 1, 3, 4, 2)) for value in outs)
        return (-minus_gains, -minus_cons, dual_whole - minus_gains + minus_cons)

    spread = P(None, "freq", None, None, None)
    return jax.shard_map(
        step,
        mesh=mesh,
        in_specs=(
            P(None, "freq", None, "bl"),
            P(None, "freq", None, None, "bl"),
            P(None, "bl"),
            P("freq", "bl"),
            spread,
            spread,
            spread,
            P(),
            P(),
        ),
        out_specs=(spread, spread, spread),
        check_vma=False,
    )
```
